512 devices in a mesh: row: 16 (over z), col: 32 (over x, y, core).
Axes of the slice: x: 4, y: 4, z: 16, core: 2. Of those that a mesh axis runs over, the one named last changes fastest.
Arguments:
- matrix_slab: float32 [6, 4096, 8192], P(None, 'row', 'col'), may hold values from 0 to 3, as said below
Outputs:
- factored: float32 [6, 4096, 8192], P(None, 'row', 'col')
The draws below stay inside these ranges and needn't reach their ends.
Inputs may be any that keep to these rules, and one draw needn't show every extreme that they name: `matrix_slab`: the first 8192 columns of a symmetric positive definite matrix: a sum of two Matern covariances of points in the plane plus a positive diagonal.
All inputs are finite; a program needn't handle non-finite values.
Results may differ from the reference program's by a relative error of at most 0.0003.
Values sent between devices are 32-bit elements; how exact they have to be, the bound alone decides.
A program may use at most 64 MiB of HBM per device.

```python
import math
import jax
import jax.numpy as jnp
from jax import lax

NB = 256
MB = 6
N_ROW = 16
N_COL = 32


def matern_kernel(rows, head, reach):
    factor = math.sqrt(3.0) / reach
    delta_x = rows[:, 0:1] - head[None, :, 0]
    delta_y = rows[:, 1:2] - head[None, :, 1]
    scaled = jnp.sqrt(delta_x * delta_x + delta_y * delta_y) * factor
    return (1.0 + scaled) * jnp.exp(-scaled)


def draw_matrix_slab(key, part):
    key = jax.random.fold_in(key, 7)
    point_key, nugget_key = jax.random.split(key)
    count = MB * N_ROW * NB
    width = N_COL * NB
    points = jax.random.uniform(point_key, (count, 2), jnp.float32)
    nugget = jax.random.uniform(nugget_key, (count,), jnp.float32, 0.5, 2.0)
    long_reach = 0.3
    short_reach = 0.03
    head = points[:width]

    def block_rows(start):
        rows = lax.dynamic_slice_in_dim(points, start, NB, 0)
        extra = lax.dynamic_slice_in_dim(nugget, start, NB, 0)
        kernel = 0.6 * matern_kernel(rows, head, long_reach) + 0.4 * matern_kernel(rows, head, short_reach)
        same = (start + jnp.arange(NB, dtype=jnp.int32))[:, None] == jnp.arange(width, dtype=jnp.int32)[None, :]
        return kernel + jnp.where(same, extra[:, None], 0.0)
    starts = jnp.arange(count // NB, dtype=jnp.int32) * NB
    blocks = lax.map(block_rows, starts)
    return blocks.reshape(MB, N_ROW * NB, width).astype(jnp.float32)


def setup_inputs(seed: int = 0) -> dict:
    key_of = jax.random.split(jax.random.key(seed), 2)
    matrix_slab = draw_matrix_slab(jax.random.fold_in(key_of[1], 71), 0)
    return dict(matrix_slab=matrix_slab)


def reference(matrix_slab):
    total = matrix_slab.shape[0] * matrix_slab.shape[1]
    width = matrix_slab.shape[2]
    count = total // NB
    ncols = width // NB
    blocks = matrix_slab.reshape(count, NB, ncols, NB)
    index = jnp.arange(count, dtype=jnp.int32)
    column_index = jnp.arange(ncols, dtype=jnp.int32)
    for step in range(2):
        lower_diag = jnp.linalg.cholesky(blocks[step, :, step, :])
        column = blocks[:, :, step, :].reshape(count * NB, NB)
        solved = jax.scipy.linalg.solve_triangular(lower_diag, column.T, lower=True).T.reshape(count, NB, NB)
        rows = index[:, None, None]
        panel = jnp.where(rows > step, solved, jnp.where(rows == step, lower_diag[None], jnp.zeros_like(solved)))
        head = panel[:ncols]
        change = jnp.einsum('iab,jcb->iajc', panel, head, precision=lax.Precision.HIGHEST)
        later = (column_index > step)[None, None, :, None]
        blocks = jnp.where(later, blocks - change, blocks)
        blocks = blocks.at[:, :, step, :].set(panel)
    keep = index[:, None, None, None] >= column_index[None, None, :, None]
    blocks = jnp.where(keep, blocks, jnp.zeros_like(blocks))
    return blocks.reshape(matrix_slab.shape)
```

```python
import functools

import jax
import jax.numpy as jnp
from jax import lax
from jax.experimental import pallas as pl
from jax.experimental.pallas import tpu as pltpu
from jax.sharding import PartitionSpec as P

HI = lax.Precision.HIGHEST
SB = 128

def dot(a, b):
    return lax.dot_general(a, b, (((1,), (0,)), ((), ())), precision=HI, preferred_element_type=jnp.float32)

def dot_nt(a, b):
    return lax.dot_general(a, b, (((1,), (1,)), ((), ())), precision=HI, preferred_element_type=jnp.float32)

def dot_tn(a, b):
    return lax.dot_general(a, b, (((0,), (0,)), ((), ())), precision=HI, preferred_element_type=jnp.float32)

def lanes(col):
    return jnp.broadcast_to(col, (8, SB))

def eliminate(strips):
    sub = lax.broadcasted_iota(jnp.int32, (8, SB), 0)
    lane = lax.broadcasted_iota(jnp.int32, (8, SB), 1)
    strips = list(strips)
    scales = []
    for k in range(16):
        cur = strips[k]
        col = [lanes(cur[:, 8 * k + j:8 * k + j + 1]) for j in range(8)]
        scale = jnp.zeros((8, SB), jnp.float32)
        rows, inner = [], []
        for j in range(8):
            pivot = lanes(col[j][j:j + 1])
            inv = 1.0 / pivot
            scale = jnp.where(sub == j, lax.rsqrt(pivot), scale)
            row = jnp.where(lane == 8 * k + j, pivot + 1.0, lanes(cur[j:j + 1])) * inv
            below = jnp.where(sub > j, col[j], 0.0)
            part = []
            for i in range(j + 1, 8):
                ratio = lanes(col[i][j:j + 1]) * inv
                col[i] = col[i] - below * ratio
                part.append(ratio)
            cur = cur - below * row
            rows.append(row)
            inner.append(part)
        strips[k] = cur
        scales.append(scale)
        for t in range(k + 1, 16):
            acc = strips[t]
            c = [lanes(acc[:, 8 * k + j:8 * k + j + 1]) for j in range(8)]
            for j in range(8):
                for i in range(j + 1, 8):
                    c[i] = c[i] - c[j] * inner[j][i - j - 1]
                acc = acc - c[j] * rows[j]
            strips[t] = acc
    return strips, scales

def factor_block(aug, xs, s):
    off = pl.multiple_of(s * SB, SB)
    strips = [aug[pl.ds(off + 8 * t, 8), pl.ds(off, SB)] for t in range(16)]
    strips, scales = eliminate(strips)
    sub = lax.broadcasted_iota(jnp.int32, (8, SB), 0)
    lane = lax.broadcasted_iota(jnp.int32, (8, SB), 1)
    for t in range(16):
        q = sub + 8 * t
        xs[8 * t:8 * t + 8, :] = jnp.where(lane < q, strips[t] * scales[t], jnp.where(lane == q, scales[t], 0.0))

def factor(aug, xs, nsb, width):
    def step(s, carry):
        off = pl.multiple_of(s * SB, SB)
        factor_block(aug, xs, s)
        x = xs[...]
        y = dot(x, aug[pl.ds(off, SB), :])
        def trail(t, c):
            toff = pl.multiple_of(t * SB, SB)
            low = dot_nt(aug[pl.ds(toff, SB), pl.ds(off, SB)], x)
            aug[pl.ds(toff, SB), :] = aug[pl.ds(toff, SB), :] - dot(low, y)
            return c
        lax.fori_loop(s + 1, nsb, trail, 0)
        aug[pl.ds(off, SB), :] = y
        return carry
    lax.fori_loop(0, nsb, step, 0)


NB = 256
N_ROW = 16
N_COL = 32
CHUNKS = 12
ROWS = 32
MESH = pl.DeviceIdType.MESH
CORNER = ((0, 0), (1, 0), (1, 1))


def send(src, dst, send_sem, recv_sem, device):
    return pltpu.make_async_remote_copy(
        src_ref=src, dst_ref=dst, send_sem=send_sem, recv_sem=recv_sem, device_id=device, device_id_type=MESH
    )


def kernel(
    x_ref, o_ref, own, corner, top, panel, aug, xs,
    own_sem, local_sem, corner_send, corner_recv, top_send, top_recv, tree_send, tree_recv, pair_send, pair_recv,
):
    row = lax.axis_index("row")
    col = lax.axis_index("col")
    core = lax.rem(col, 2)
    y = lax.rem(col // 2, 4)
    x = col // 8
    is_root = col < 2

    own_copy = pltpu.make_async_copy(x_ref, own, own_sem)
    own_copy.start()
    barrier = pltpu.get_barrier_semaphore()

    def greet_col(c, carry):
        @pl.when(c != col)
        def _():
            pl.semaphore_signal(barrier, inc=1, device_id=(row, c), device_id_type=MESH)
        return carry

    def greet_row(r, carry):
        @pl.when(r != row)
        def _():
            pl.semaphore_signal(barrier, inc=1, device_id=(r, col), device_id_type=MESH)
        return carry

    lax.fori_loop(0, N_COL, greet_col, 0)
    lax.fori_loop(0, N_ROW, greet_row, 0)
    own_copy.wait()

    @pl.when(is_root)
    def _():
        c0 = pltpu.make_async_copy(own, panel.at[core], local_sem.at[0])
        c0.start()
        c0.wait()

    for b, (hr, hc) in enumerate(CORNER):
        @pl.when((row == hr) & (col == hc))
        def _():
            c1 = pltpu.make_async_copy(own.at[0], corner.at[b], local_sem.at[1])
            c1.start()
            c1.wait()

    @pl.when(row < 2)
    def _():
        c2 = pltpu.make_async_copy(own.at[0], top.at[row], local_sem.at[2])
        c2.start()
        c2.wait()

    pl.semaphore_wait(barrier, N_COL + N_ROW - 2)

    def strip(b, c):
        return corner.at[b, pl.ds(pl.multiple_of(c * 8, 8), 8), :]

    def strips(b, n):
        return corner.at[b, pl.ds(0, 8 * n), :]

    def each(n, me, body):
        def one(i, carry):
            @pl.when(i != me)
            def _():
                body(i)
            return carry
        lax.fori_loop(0, n, one, 0)

    for b, (hr, hc) in enumerate(CORNER):
        @pl.when((row == hr) & (col == hc))
        def _():
            each(N_COL, col, lambda c: send(
                strip(b, c), strip(b, c), corner_send.at[0, b], corner_recv.at[0, b], (row, c)).start())

    for b, (hr, hc) in enumerate(CORNER):
        mine = strip(b, col)

        @pl.when((row == hr) & (col != hc))
        def _():
            send(mine, mine, corner_send.at[0, b], corner_recv.at[0, b], (row, col)).wait_recv()

        @pl.when(row == hr)
        def _():
            each(N_ROW, row, lambda r: send(
                mine, mine, corner_send.at[1, b], corner_recv.at[1, b], (r, col)).start())

        @pl.when(row != hr)
        def _():
            send(mine, mine, corner_send.at[1, b], corner_recv.at[1, b], (row, col)).wait_recv()

        def spread(c):
            @pl.when((row != hr) | (c != hc))
            def _():
                send(mine, mine, corner_send.at[2, b], corner_recv.at[2, b], (row, c)).start()
        each(N_COL, col, spread)

    def rounds(t, carry):
        for q in range(2):
            delta = lax.rem(row - q + N_ROW, N_ROW)
            depth = jnp.where(delta <= 8, delta, N_ROW - delta)
            m = t - depth
            piece = top.at[q, pl.ds(pl.multiple_of(jnp.clip(m, 0, 3) * 64, 64), 64), :]
            slot = jnp.clip(m, 0, 3)

            @pl.when((m >= 0) & (m < 4))
            def _():
                @pl.when(delta > 0)
                def _():
                    send(piece, piece, top_send.at[q, 0], top_recv.at[q, slot], (row, col)).wait_recv()

                @pl.when(delta < 8)
                def _():
                    send(piece, piece, top_send.at[q, 0], top_recv.at[q, slot],
                         (lax.rem(row + 1, N_ROW), col)).start()

                @pl.when((delta == 0) | (delta >= 10))
                def _():
                    send(piece, piece, top_send.at[q, 1], top_recv.at[q, slot],
                         (lax.rem(row + N_ROW - 1, N_ROW), col)).start()

        for tree in range(4):
            u, v, step_u, step_v = (
                (x, y, (1, 0), (0, 1)),
                (y, lax.rem(4 - x, 4), (0, 1), (3, 0)),
                (lax.rem(4 - x, 4), lax.rem(4 - y, 4), (3, 0), (0, 3)),
                (lax.rem(4 - y, 4), x, (0, 3), (1, 0)),
            )[tree]
            depth = jnp.where(v == 0, u, jnp.where(u >= 1, u + v, v + 4))
            m = t - depth
            slot = jnp.clip(m, 0, CHUNKS - 1)
            piece = panel.at[core, slot // 2, pl.ds(pl.multiple_of(64 * tree + 32 * lax.rem(slot, 2), 32), ROWS), :]

            def at(step):
                return (row, lax.rem(x + step[0], 4) * 8 + lax.rem(y + step[1], 4) * 2 + core)

            @pl.when((m >= 0) & (m < CHUNKS))
            def _():
                @pl.when((u != 0) | (v != 0))
                def _():
                    send(piece, piece, tree_send.at[tree, 0], tree_recv.at[tree, slot], (row, col)).wait_recv()

                @pl.when(((v == 0) & (u <= 2)) | ((v >= 1) & (u == 3)))
                def _():
                    send(piece, piece, tree_send.at[tree, 0], tree_recv.at[tree, slot], at(step_u)).start()

                @pl.when((u >= 1) & (v <= 2))
                def _():
                    send(piece, piece, tree_send.at[tree, 1], tree_recv.at[tree, slot], at(step_v)).start()

                send(piece, piece, pair_send, pair_recv, (row, col + 1 - 2 * core)).start()
        return carry

    lax.fori_loop(0, CHUNKS + 7, rounds, 0)

    for b, (hr, hc) in enumerate(CORNER):
        @pl.when((row != hr) | (col != hc))
        def _():
            send(strips(b, 31), strips(b, 31), corner_send.at[2, b], corner_recv.at[2, b], (row, col)).wait_recv()
    send(panel.at[1 - core], panel.at[1 - core], pair_send, pair_recv, (row, col)).wait_recv()

    aug[0:256, 0:256] = corner[0]
    aug[256:512, 0:256] = corner[1]
    aug[0:256, 256:512] = corner[1].T
    aug[256:512, 256:512] = corner[2]
    aug[0:256, 512:768] = top[0]
    aug[256:512, 512:768] = top[1]
    wide_r = lax.broadcasted_iota(jnp.int32, (512, 512), 0)
    wide_c = lax.broadcasted_iota(jnp.int32, (512, 512), 1)
    aug[:, 768:1280] = jnp.where(wide_r == wide_c, 1.0, 0.0)
    factor(aug, xs, 4, 1280)
    tall_r = lax.broadcasted_iota(jnp.int32, (512, 256), 0)
    tall_c = lax.broadcasted_iota(jnp.int32, (512, 256), 1)
    pick = jnp.where(tall_r == tall_c + NB * col, -1.0, 0.0)
    rhs = jnp.where(is_root, pick, aug[:, 512:768])
    aug[:, 512:768] = dot_tn(aug[:, 768:1280], rhs)

    sq_r = lax.broadcasted_iota(jnp.int32, (NB, NB), 0)
    sq_c = lax.broadcasted_iota(jnp.int32, (NB, NB), 1)

    def update(g, carry):
        index = g * N_ROW + row
        change = dot(panel[0, g], aug[0:256, 512:768]) + dot(panel[1, g], aug[256:512, 512:768])
        value = jnp.where(is_root, 0.0, own[g]) - change
        keep = (index > col) | ((index == col) & ((sq_r >= sq_c) | jnp.logical_not(is_root)))
        o_ref[g] = jnp.where(keep, value, 0.0)
        return carry

    lax.fori_loop(0, 6, update, 0)

    for b, (hr, hc) in enumerate(CORNER):
        @pl.when((row == hr) & (col == hc))
        def _():
            send(strips(b, 31), strips(b, 31), corner_send.at[0, b], corner_recv.at[0, b], (row, col)).wait_send()

        @pl.when(row == hr)
        def _():
            send(strips(b, 15), strips(b, 15), corner_send.at[1, b], corner_recv.at[1, b], (row, col)).wait_send()

        @pl.when((row == hr) & (col != hc))
        def _():
            send(strips(b, 30), strips(b, 30), corner_send.at[2, b], corner_recv.at[2, b], (row, col)).wait_send()

        @pl.when((row != hr) | (col == hc))
        def _():
            send(strips(b, 31), strips(b, 31), corner_send.at[2, b], corner_recv.at[2, b], (row, col)).wait_send()

    for q in range(2):
        delta = lax.rem(row - q + N_ROW, N_ROW)
        whole = top.at[q]

        @pl.when(delta < 8)
        def _():
            send(whole, whole, top_send.at[q, 0], top_recv.at[q, 0], (row, col)).wait_send()

        @pl.when((delta == 0) | (delta >= 10))
        def _():
            send(whole, whole, top_send.at[q, 1], top_recv.at[q, 0], (row, col)).wait_send()

    for tree in range(4):
        u, v = (
            (x, y), (y, lax.rem(4 - x, 4)), (lax.rem(4 - x, 4), lax.rem(4 - y, 4)), (lax.rem(4 - y, 4), x),
        )[tree]
        part = panel.at[core, :, pl.ds(64 * tree, 64), :]

        @pl.when(((v == 0) & (u <= 2)) | ((v >= 1) & (u == 3)))
        def _():
            send(part, part, tree_send.at[tree, 0], tree_recv.at[tree, 0], (row, col)).wait_send()

        @pl.when((u >= 1) & (v <= 2))
        def _():
            send(part, part, tree_send.at[tree, 1], tree_recv.at[tree, 0], (row, col)).wait_send()
    send(panel.at[core], panel.at[core], pair_send, pair_recv, (row, col)).wait_send()


def on_device(slab):
    return pl.pallas_call(
        kernel,
        out_shape=jax.ShapeDtypeStruct(slab.shape, jnp.float32),
        in_specs=[pl.BlockSpec(memory_space=pl.ANY)],
        out_specs=pl.BlockSpec(memory_space=pltpu.VMEM),
        scratch_shapes=[
            pltpu.VMEM((6, NB, NB), jnp.float32),
            pltpu.VMEM((3, NB, NB), jnp.float32),
            pltpu.VMEM((2, NB, NB), jnp.float32),
            pltpu.VMEM((2, 6, NB, NB), jnp.float32),
            pltpu.VMEM((512, 1280), jnp.float32),
            pltpu.VMEM((SB, SB), jnp.float32),
            pltpu.SemaphoreType.DMA,
            pltpu.SemaphoreType.DMA((3,)),
            pltpu.SemaphoreType.DMA((3, 3)),
            pltpu.SemaphoreType.DMA((3, 3)),
            pltpu.SemaphoreType.DMA((2, 2)),
            pltpu.SemaphoreType.DMA((2, 4)),
            pltpu.SemaphoreType.DMA((4, 2)),
            pltpu.SemaphoreType.DMA((4, CHUNKS)),
            pltpu.SemaphoreType.DMA,
            pltpu.SemaphoreType.DMA,
        ],
        compiler_params=pltpu.CompilerParams(
            collective_id=0, has_side_effects=True, vmem_limit_bytes=48 * 2**20
        ),
    )(slab)


def solution(mesh):
    spec = P(None, "row", "col")
    return jax.shard_map(on_device, mesh=mesh, in_specs=(spec,), out_specs=spec, check_vma=False)
```

```python
import jax
import jax.numpy as jnp
from jax import lax
from jax.experimental import pallas as pl
from jax.experimental.pallas import tpu as pltpu
from jax.sharding import PartitionSpec as P

HI = lax.Precision.HIGHEST
SB = 128

def dot(a, b):
    return lax.dot_general(a, b, (((1,), (0,)), ((), ())), precision=HI, preferred_element_type=jnp.float32)

def dot_nt(a, b):
    return lax.dot_general(a, b, (((1,), (1,)), ((), ())), precision=HI, preferred_element_type=jnp.float32)

def dot_tn(a, b):
    return lax.dot_general(a, b, (((0,), (0,)), ((), ())), precision=HI, preferred_element_type=jnp.float32)

def lanes(col):
    return jnp.broadcast_to(col, (8, SB))

def eliminate(strips, after):
    sub = lax.broadcasted_iota(jnp.int32, (8, SB), 0)
    lane = lax.broadcasted_iota(jnp.int32, (8, SB), 1)
    strips = list(strips)
    scales = []
    for k in range(16):
        cur = strips[k]
        col = [lanes(cur[:, 8 * k + j:8 * k + j + 1]) for j in range(8)]
        scale = jnp.zeros((8, SB), jnp.float32)
        rows, inner = [], []
        for j in range(8):
            pivot = lanes(col[j][j:j + 1])
            inv = 1.0 / pivot
            scale = jnp.where(sub == j, lax.rsqrt(pivot), scale)
            row = jnp.where(lane == 8 * k + j, pivot + 1.0, lanes(cur[j:j + 1])) * inv
            below = jnp.where(sub > j, col[j], 0.0)
            part = []
            for i in range(j + 1, 8):
                ratio = lanes(col[i][j:j + 1]) * inv
                col[i] = col[i] - below * ratio
                part.append(ratio)
            cur = cur - below * row
            rows.append(row)
            inner.append(part)
        strips[k] = cur
        scales.append(scale)
        for t in range(k + 1, 16):
            acc = strips[t]
            c = [lanes(acc[:, 8 * k + j:8 * k + j + 1]) for j in range(8)]
            for j in range(8):
                for i in range(j + 1, 8):
                    c[i] = c[i] - c[j] * inner[j][i - j - 1]
                acc = acc - c[j] * rows[j]
            strips[t] = acc
        after(k)
    return strips, scales


NB = 256
N_ROW = 16
N_COL = 32
MESH = pl.DeviceIdType.MESH
TREE_PARTS = 12
TOP_PARTS = 8
SKEW = 3
EARLY = 3


def send(src, dst, send_sem, recv_sem, device):
    return pltpu.make_async_remote_copy(
        src_ref=src, dst_ref=dst, send_sem=send_sem, recv_sem=recv_sem, device_id=device, device_id_type=MESH
    )


def kernel(
    x_ref, o_ref, own, first, low, high, top, panel, aug, xs,
    own_sem, scatter_send, scatter_recv, ring_send, ring_recv, plane_send, plane_recv, twin_send, twin_recv,
    top_send, top_recv, tree_send, tree_recv, pair_send, pair_recv,
):
    row = lax.axis_index("row")
    col = lax.axis_index("col")
    core = lax.rem(col, 2)
    chip = col // 2
    x = chip // 4
    y = lax.rem(chip, 4)
    is_root = col < 2
    twin = (row, col + 1 - 2 * core)
    here = (row, col)

    own_copy = pltpu.make_async_copy(x_ref, own, own_sem)
    own_copy.start()

    def loop(n, body):
        def one(i, carry):
            body(i)
            return carry
        lax.fori_loop(0, n, one, 0)

    def plane_peer(j):
        o = 10 + j
        o = jnp.where(o >= 16, o - 15, o)
        return lax.rem(x + o // 4, 4) * 4 + lax.rem(y + lax.rem(o, 4), 4)

    def ring_peer(j):
        half = (j + 1) // 2
        return lax.rem(row + 8 + jnp.where(lax.rem(j, 2) == 1, -half, half) + N_ROW, N_ROW)

    barrier = pltpu.get_barrier_semaphore()
    loop(15, lambda j: pl.semaphore_signal(barrier, inc=1, device_id=(ring_peer(j), col), device_id_type=MESH))
    loop(15, lambda j: pl.semaphore_signal(
        barrier, inc=1, device_id=(row, plane_peer(j) * 2 + core), device_id_type=MESH))
    pl.semaphore_signal(barrier, inc=1, device_id=twin, device_id_type=MESH)
    own_copy.wait()

    def first_piece(i):
        return first.at[pl.ds(pl.multiple_of(i * 8, 8), 8), :]

    holds_00 = (row == 0) & (col == 0)
    holds_10 = (row == 1) & (col == 0)
    holds_11 = (row == 1) & (col == 1)

    @pl.when(holds_00)
    def _():
        first[0:8, :] = own[0, 0:8, 0:SB]
        low[0, 0:8, :] = own[0, SB:SB + 8, :]

    @pl.when(holds_10)
    def _():
        low[0, 8:24, :] = own[0, 0:16, :]

    @pl.when(holds_11)
    def _():
        high[0] = own[0, 0:16, :]

    @pl.when(is_root)
    def _():
        panel[core] = own[...]

    @pl.when(row < 2)
    def _():
        top[row] = own[0]

    pl.semaphore_wait(barrier, 31)

    def own_rows(start, n):
        return own.at[0, pl.ds(pl.multiple_of(start, 8), n), :]

    @pl.when(holds_00)
    def _():
        loop(15, lambda j: send(
            own.at[0, pl.ds(pl.multiple_of(plane_peer(j) * 8, 8), 8), pl.ds(0, SB)], first_piece(plane_peer(j)),
            scatter_send.at[0], scatter_recv.at[0], (row, plane_peer(j) * 2)).start())
        loop(15, lambda j: send(
            own_rows(SB + plane_peer(j) * 8, 8), low.at[plane_peer(j), pl.ds(0, 8), :],
            scatter_send.at[1], scatter_recv.at[1], (row, plane_peer(j) * 2)).start())

    @pl.when(holds_10)
    def _():
        loop(15, lambda j: send(
            own_rows(plane_peer(j) * 16, 16), low.at[plane_peer(j), pl.ds(8, 16), :],
            scatter_send.at[2], scatter_recv.at[2], (row, plane_peer(j) * 2)).start())

    @pl.when(holds_11)
    def _():
        loop(15, lambda j: send(
            own_rows(plane_peer(j) * 16, 16), high.at[plane_peer(j)],
            scatter_send.at[3], scatter_recv.at[3], (row, plane_peer(j) * 2 + 1)).start())

    pieces = (
        (first_piece(chip), 0, 0),
        (low.at[chip, pl.ds(0, 8), :], 0, 0),
        (low.at[chip, pl.ds(8, 16), :], 1, 0),
        (high.at[chip], 1, 1),
    )
    for n, (piece, start, carrier) in enumerate(pieces):
        @pl.when((row == start) & (core == carrier))
        def _():
            @pl.when(chip != 0)
            def _():
                send(piece, piece, scatter_send.at[n], scatter_recv.at[n], here).wait_recv()
            loop(15, lambda j: send(
                piece, piece, ring_send.at[n], ring_recv.at[n], (ring_peer(j), col)).start())

    def ring_arrived(n):
        piece, start, _ = pieces[n]

        @pl.when(row != start)
        def _():
            send(piece, piece, ring_send.at[n], ring_recv.at[n], here).wait_recv()

    @pl.when(core == 0)
    def _():
        ring_arrived(0)
        loop(15, lambda j: send(
            first_piece(chip), first_piece(chip), plane_send.at[0], plane_recv.at[0],
            (row, plane_peer(j) * 2)).start())
        ring_arrived(1)
        ring_arrived(2)
        loop(15, lambda j: send(
            low.at[chip], low.at[chip], plane_send.at[1], plane_recv.at[1], (row, plane_peer(j) * 2)).start())

    @pl.when(core == 1)
    def _():
        ring_arrived(3)
        loop(15, lambda j: send(
            high.at[chip], high.at[chip], plane_send.at[2], plane_recv.at[2],
            (row, plane_peer(j) * 2 + 1)).start())

    q = lax.rem(row, 2)
    delta = row - q
    top_depth = jnp.where(delta <= 8, delta, N_ROW - delta) // 2

    def top_to(offset):
        return (lax.rem(row + offset + N_ROW, N_ROW), col)

    def top_step(t):
        m = t - SKEW * top_depth
        slot = jnp.clip(m, 0, TOP_PARTS - 1)
        piece = top.at[q, pl.ds(pl.multiple_of(slot * 32, 32), 32), :]

        def go(kind, offset):
            send(piece, piece, top_send.at[kind], top_recv.at[q, slot], top_to(offset)).start()

        @pl.when((m >= 0) & (m < TOP_PARTS))
        def _():
            @pl.when(delta > 0)
            def _():
                send(piece, piece, top_send.at[0], top_recv.at[q, slot], here).wait_recv()

            @pl.when(delta < 8)
            def _():
                go(0, 2)

            @pl.when((delta == 0) | (delta >= 12))
            def _():
                go(1, -2)

            @pl.when((delta >= 2) & (delta <= 8))
            def _():
                go(2, -1)

            @pl.when(delta >= 8)
            def _():
                go(3, 1)

    def hops(p):
        return jnp.where(p == 0, 0, jnp.where(p == 2, 2, 1))

    def tree_step(t):
        for h in range(2):
            u, v = (x, y) if h == 0 else (y, x)
            p = jnp.where(v == 0, u, v)

            def at(u2, v2):
                x2, y2 = (u2, v2) if h == 0 else (v2, u2)
                return (row, x2 * 8 + y2 * 2 + core)

            m = t - SKEW * (hops(u) + hops(v))
            slot = jnp.clip(m, 0, TREE_PARTS - 1)
            start = 128 * h + 64 * lax.rem(slot, 2)
            part = panel.at[core, slot // 2, pl.ds(pl.multiple_of(start, 64), 64), :]
            half0 = panel.at[core, slot // 2, pl.ds(pl.multiple_of(start, 32), 32), :]
            half1 = panel.at[core, slot // 2, pl.ds(pl.multiple_of(start + 32, 32), 32), :]

            def go(piece, kind, half, device):
                send(piece, piece, tree_send.at[h, kind], tree_recv.at[h, slot, half], device).start()

            @pl.when((m >= 0) & (m < TREE_PARTS))
            def _():
                @pl.when((p == 1) | (p == 3))
                def _():
                    send(part, part, tree_send.at[h, 0], tree_recv.at[h, slot, 0], here).wait_recv()

                @pl.when(p == 2)
                def _():
                    send(half0, half0, tree_send.at[h, 0], tree_recv.at[h, slot, 0], here).wait_recv()
                    send(half1, half1, tree_send.at[h, 0], tree_recv.at[h, slot, 1], here).wait_recv()

                @pl.when((v == 0) & (u == 0))
                def _():
                    go(part, 0, 0, at(1, 0))
                    go(part, 1, 0, at(3, 0))

                @pl.when(p == 1)
                def _():
                    go(half0, 2, 0, at(jnp.where(v == 0, 2, u), jnp.where(v == 0, 0, 2)))

                @pl.when(p == 3)
                def _():
                    go(half1, 2, 1, at(jnp.where(v == 0, 2, u), jnp.where(v == 0, 0, 2)))

                @pl.when(v == 0)
                def _():
                    go(part, 3, 0, at(u, 1))
                    go(part, 4, 0, at(u, 3))

                send(part, part, pair_send.at[h], pair_recv.at[h], twin).start()

    def tick(t):
        top_step(t)
        tree_step(t)

    for t in range(EARLY):
        tick(jnp.int32(t))

    @pl.when(core == 0)
    def _():
        send(first.at[pl.ds(0, 120), :], first.at[pl.ds(0, 120), :], plane_send.at[0], plane_recv.at[0], here).wait_recv()
        send(first, first, twin_send.at[0], twin_recv.at[0], twin).start()

    @pl.when(core == 1)
    def _():
        send(first, first, twin_send.at[0], twin_recv.at[0], here).wait_recv()

    def rest_in_plane():
        @pl.when(core == 0)
        def _():
            send(low.at[pl.ds(0, 15)], low.at[pl.ds(0, 15)], plane_send.at[1], plane_recv.at[1], here).wait_recv()
            send(low, low, twin_send.at[1], twin_recv.at[1], twin).start()

        @pl.when(core == 1)
        def _():
            send(high.at[pl.ds(0, 15)], high.at[pl.ds(0, 15)], plane_send.at[2], plane_recv.at[2], here).wait_recv()
            send(high, high, twin_send.at[2], twin_recv.at[2], twin).start()

    def rest_from_twin():
        @pl.when(core == 1)
        def _():
            send(low, low, twin_send.at[1], twin_recv.at[1], here).wait_recv()

        @pl.when(core == 0)
        def _():
            send(high, high, twin_send.at[2], twin_recv.at[2], here).wait_recv()

        for i in range(16):
            aug[SB + 8 * i:SB + 8 * i + 8, 0:NB] = low[i, 0:8, :]
            aug[NB + 16 * i:NB + 16 * i + 16, 0:NB] = low[i, 8:24, :]
            aug[NB + 16 * i:NB + 16 * i + 16, NB:2 * NB] = high[i]
        aug[0:SB, SB:NB] = aug[SB:NB, 0:SB].T
        aug[0:NB, NB:2 * NB] = aug[NB:2 * NB, 0:NB].T

    wide_r = lax.broadcasted_iota(jnp.int32, (512, 512), 0)
    wide_c = lax.broadcasted_iota(jnp.int32, (512, 512), 1)
    aug[:, 512:1024] = jnp.where(wide_r == wide_c, 1.0, 0.0)
    aug[0:SB, 0:SB] = first[...]
    sub = lax.broadcasted_iota(jnp.int32, (8, SB), 0)
    lane = lax.broadcasted_iota(jnp.int32, (8, SB), 1)

    def factor_step(s, carry):
        off = pl.multiple_of(s * SB, SB)

        def after(k):
            if k % 3 == 2:
                if k == 8:
                    pl.when(s == 0)(rest_in_plane)
                tick(EARLY + 6 * s + k // 3)

        strips, scales = eliminate([aug[pl.ds(off + 8 * t, 8), pl.ds(off, SB)] for t in range(16)], after)
        for t in range(16):
            diag = sub + 8 * t
            xs[8 * t:8 * t + 8, :] = jnp.where(
                lane < diag, strips[t] * scales[t], jnp.where(lane == diag, scales[t], 0.0))
        pl.when(s == 0)(rest_from_twin)
        inverse = xs[...]
        done = dot(inverse, aug[pl.ds(off, SB), :])

        def trail(t, c):
            toff = pl.multiple_of(t * SB, SB)
            lower = dot_nt(aug[pl.ds(toff, SB), pl.ds(off, SB)], inverse)
            aug[pl.ds(toff, SB), :] = aug[pl.ds(toff, SB), :] - dot(lower, done)
            return c
        lax.fori_loop(s + 1, 4, trail, 0)
        aug[pl.ds(off, SB), :] = done
        tick(EARLY + 6 * s + 5)
        return carry

    lax.fori_loop(0, 4, factor_step, 0)

    def top_arrived(m):
        piece = top.at[1 - q, pl.ds(pl.multiple_of(m * 32, 32), 32), :]
        send(piece, piece, top_send.at[0], top_recv.at[1 - q, m], here).wait_recv()

    @pl.when((row != 0) | (q != 1))
    def _():
        loop(TOP_PARTS, top_arrived)

    tall_r = lax.broadcasted_iota(jnp.int32, (512, NB), 0)
    tall_c = lax.broadcasted_iota(jnp.int32, (512, NB), 1)
    solved = dot(aug[:, 512:768], top[0]) + dot(aug[:, 768:1024], top[1])
    aug[:, 0:NB] = jnp.where(is_root, jnp.where(tall_r == tall_c + NB * col, -1.0, 0.0), solved)
    aug[:, NB:2 * NB] = dot_tn(aug[:, 512:1024], aug[:, 0:NB])

    for h in range(2):
        part = panel.at[1 - core, :, pl.ds(128 * h, 128), :]
        send(part, part, pair_send.at[h], pair_recv.at[h], here).wait_recv()

    sq_r = lax.broadcasted_iota(jnp.int32, (NB, NB), 0)
    sq_c = lax.broadcasted_iota(jnp.int32, (NB, NB), 1)

    def update(g):
        index = g * N_ROW + row
        change = dot(panel[0, g], aug[0:NB, NB:2 * NB]) + dot(panel[1, g], aug[NB:2 * NB, NB:2 * NB])
        value = jnp.where(is_root, 0.0, own[g]) - change
        keep = (index > col) | ((index == col) & ((sq_r >= sq_c) | jnp.logical_not(is_root)))
        o_ref[g] = jnp.where(keep, value, 0.0)

    loop(6, update)

    def sent(ref, sem):
        send(ref, ref, sem, own_sem, here).wait_send()

    for n, holds, ref in (
        (0, holds_00, first.at[pl.ds(0, 120), :]),
        (1, holds_00, low.at[pl.ds(0, 15), pl.ds(0, 8), :]),
        (2, holds_10, low.at[pl.ds(0, 15), pl.ds(8, 16), :]),
        (3, holds_11, high.at[pl.ds(0, 15)]),
    ):
        pl.when(holds)(lambda n=n, ref=ref: sent(ref, scatter_send.at[n]))
        pl.when((row == pieces[n][1]) & (core == pieces[n][2]))(lambda n=n, ref=ref: sent(ref, ring_send.at[n]))

    @pl.when(core == 0)
    def _():
        sent(first.at[pl.ds(0, 120), :], plane_send.at[0])
        sent(low.at[pl.ds(0, 15)], plane_send.at[1])
        sent(first, twin_send.at[0])
        sent(low, twin_send.at[1])

    @pl.when(core == 1)
    def _():
        sent(high.at[pl.ds(0, 15)], plane_send.at[2])
        sent(high, twin_send.at[2])

    pl.when(delta < 8)(lambda: sent(top.at[0], top_send.at[0]))
    pl.when((delta == 0) | (delta >= 12))(lambda: sent(top.at[0], top_send.at[1]))
    pl.when((delta >= 2) & (delta <= 8))(lambda: sent(top.at[0], top_send.at[2]))
    pl.when(delta >= 8)(lambda: sent(top.at[0], top_send.at[3]))

    for h in range(2):
        u, v = (x, y) if h == 0 else (y, x)
        p = jnp.where(v == 0, u, v)
        whole = panel.at[core, :, pl.ds(0, 128), :]
        half = panel.at[core, :, pl.ds(0, 64), :]

        @pl.when((v == 0) & (u == 0))
        def _():
            sent(whole, tree_send.at[h, 0])
            sent(whole, tree_send.at[h, 1])

        pl.when((p == 1) | (p == 3))(lambda: sent(half, tree_send.at[h, 2]))

        @pl.when(v == 0)
        def _():
            sent(whole, tree_send.at[h, 3])
            sent(whole, tree_send.at[h, 4])

        sent(whole, pair_send.at[h])


def on_device(slab):
    dma = pltpu.SemaphoreType.DMA
    return pl.pallas_call(
        kernel,
        out_shape=jax.ShapeDtypeStruct(slab.shape, jnp.float32),
        in_specs=[pl.BlockSpec(memory_space=pl.ANY)],
        out_specs=pl.BlockSpec(memory_space=pltpu.VMEM),
        scratch_shapes=[
            pltpu.VMEM((6, NB, NB), jnp.float32),
            pltpu.VMEM((SB, SB), jnp.float32),
            pltpu.VMEM((16, 24, NB), jnp.float32),
            pltpu.VMEM((16, 16, NB), jnp.float32),
            pltpu.VMEM((2, NB, NB), jnp.float32),
            pltpu.VMEM((2, 6, NB, NB), jnp.float32),
            pltpu.VMEM((512, 1024), jnp.float32),
            pltpu.VMEM((SB, SB), jnp.float32),
            dma, dma((4,)), dma((4,)), dma((4,)), dma((4,)), dma((3,)), dma((3,)), dma((3,)), dma((3,)),
            dma((4,)), dma((2, TOP_PARTS)), dma((2, 5)), dma((2, TREE_PARTS, 2)), dma((2,)), dma((2,)),
        ],
        compiler_params=pltpu.CompilerParams(
            collective_id=0, has_side_effects=True, vmem_limit_bytes=60 * 2**20
        ),
    )(slab)


def solution(mesh):
    spec = P(None, "row", "col")
    return jax.shard_map(on_device, mesh=mesh, in_specs=(spec,), out_specs=spec, check_vma=False)
```

```python
import jax
import jax.numpy as jnp
from jax import lax
from jax.experimental import pallas as pl
from jax.experimental.pallas import tpu as pltpu
from jax.sharding import PartitionSpec as P

HI = lax.Precision.HIGHEST
SB = 128


def contract(a, b, da, db):
    return lax.dot_general(a, b, (((da,), (db,)), ((), ())), precision=HI, preferred_element_type=jnp.float32)


def dot(a, b):
    return contract(a, b, 1, 0)


def dot_nt(a, b):
    return contract(a, b, 1, 1)


def dot_tn(a, b):
    return contract(a, b, 0, 0)


def lanes(part):
    return jnp.broadcast_to(part, (8, SB))


def eliminate(strips, after):
    sub = lax.broadcasted_iota(jnp.int32, (8, SB), 0)
    lane = lax.broadcasted_iota(jnp.int32, (8, SB), 1)
    strips = list(strips)
    scales = []
    for k in range(16):
        cur = strips[k]
        col = [lanes(cur[:, 8 * k + j:8 * k + j + 1]) for j in range(8)]
        scale = jnp.zeros((8, SB), jnp.float32)
        pairs = []
        for j in range(0, 8, 2):
            a = lanes(col[j][j:j + 1])
            b = lanes(col[j][j + 1:j + 2])
            c = lanes(col[j + 1][j + 1:j + 2])
            det = a * c - b * b
            inv = 1.0 / det
            over_a = 1.0 / a
            scale = jnp.where(sub == j, lax.rsqrt(a), jnp.where(sub == j + 1, lax.rsqrt(det * over_a), scale))
            low0 = jnp.where(sub > j + 1, col[j], 0.0)
            low1 = jnp.where(sub > j + 1, col[j + 1], 0.0)

            def solve(r0, r1):
                return (c * r0 - b * r1) * inv, (a * r1 - b * r0) * inv

            ratios = []
            for i in range(j + 2, 8):
                u, w = solve(lanes(col[i][j:j + 1]), lanes(col[i][j + 1:j + 2]))
                col[i] = col[i] - low0 * u - low1 * w
                ratios.append((u, w))
            r0 = jnp.where(lane == 8 * k + j, a + 1.0, lanes(cur[j:j + 1]))
            r1 = jnp.where(lane == 8 * k + j + 1, c + 1.0, lanes(cur[j + 1:j + 2]))
            u, w = solve(r0, r1)
            cur = cur - low0 * u - low1 * w - jnp.where(sub == j + 1, b * over_a, 0.0) * r0
            pairs.append((ratios, u, w))
        strips[k] = cur
        scales.append(scale)
        for t in range(k + 1, 16):
            acc = strips[t]
            c = [lanes(acc[:, 8 * k + j:8 * k + j + 1]) for j in range(8)]
            for p, (ratios, u, w) in enumerate(pairs):
                c0, c1 = c[2 * p], c[2 * p + 1]
                for i, (ui, wi) in enumerate(ratios):
                    c[2 * p + 2 + i] = c[2 * p + 2 + i] - c0 * ui - c1 * wi
                acc = acc - c0 * u - c1 * w
            strips[t] = acc
        after(k)
    return strips, scales


def block(i):
    return pl.ds(pl.multiple_of(i * SB, SB), SB)


def factor(a, m, z, lb, xs, hook, unpack):
    sub = lax.broadcasted_iota(jnp.int32, (8, SB), 0)
    lane = lax.broadcasted_iota(jnp.int32, (8, SB), 1)
    xs[...] = jnp.zeros((SB, SB), jnp.float32)
    lb[...] = jnp.zeros((3, SB, SB), jnp.float32)

    def step(s, carry):
        p = jnp.maximum(s - 1, 0)

        def lower(i):
            lb[i] = dot_nt(a[block(s + i), block(p)], xs[...])

        def schur(i, j):
            a[block(s + i), block(s + j)] = a[block(s + i), block(s + j)] - dot_nt(lb[i], lb[j])

        def rows():
            z[block(p), :] = dot(xs[...], m[block(p), :])

        def spread(i):
            m[block(s + i), :] = m[block(s + i), :] - dot(lb[i], z[block(p), :])

        jobs = {
            0: (lambda: lower(1), lambda: lower(2)),
            1: (rows,),
            3: (lambda: schur(1, 0), lambda: schur(1, 1)),
            4: (lambda: schur(2, 0), lambda: schur(2, 1)),
            5: (lambda: schur(2, 2),),
            6: (lambda: spread(0),),
            9: (lambda: spread(1),),
            12: (lambda: spread(2),),
        }

        def after(k):
            for job in jobs.get(k, ()):
                job()
            hook(s, k)

        strips, scales = eliminate([a[pl.ds(pl.multiple_of(s * SB + 8 * t, 8), 8), block(s)] for t in range(16)], after)
        unpack(s)
        for t in range(16):
            diag = sub + 8 * t
            xs[8 * t:8 * t + 8, :] = jnp.where(
                lane < diag, strips[t] * scales[t], jnp.where(lane == diag, scales[t], 0.0))
        lb[0] = dot_nt(a[block(s + 1), block(s)], xs[...])
        a[block(s + 1), block(s + 1)] = a[block(s + 1), block(s + 1)] - dot_nt(lb[0], lb[0])
        return carry

    lax.fori_loop(0, 4, step, 0)
    z[block(3), :] = dot(xs[...], m[block(3), :])

NB = 256
N_ROW = 16
N_COL = 32
MESH = pl.DeviceIdType.MESH
TREE_PARTS = 12
TOP_PARTS = 8
SKEW = 5
EARLY = 10
VMEM = 28 * 2**20


def halves(v):
    hi = v.astype(jnp.bfloat16)
    return hi, (v - hi.astype(jnp.float32)).astype(jnp.bfloat16)


def dot16(p, q):
    return lax.dot_general(p, q, (((1,), (0,)), ((), ())), preferred_element_type=jnp.float32)


def send(src, dst, send_sem, recv_sem, device):
    return pltpu.make_async_remote_copy(
        src_ref=src, dst_ref=dst, send_sem=send_sem, recv_sem=recv_sem, device_id=device, device_id_type=MESH
    )


def kernel(
    x_ref, o_ref, own, first, low, high, top, panel, a, m, z, lb, xs, w_hi, w_lo,
    own_sem, scatter_send, scatter_recv, ring_send, ring_recv, plane_send, plane_recv, twin_send, twin_recv,
    top_send, top_recv, tree_send, tree_recv, pair_send, pair_recv,
):
    row = lax.axis_index("row")
    col = lax.axis_index("col")
    core = lax.rem(col, 2)
    chip = col // 2
    x = chip // 4
    y = lax.rem(chip, 4)
    is_root = col < 2
    twin = (row, col + 1 - 2 * core)
    here = (row, col)

    own_copy = pltpu.make_async_copy(x_ref, own, own_sem)
    own_copy.start()

    def loop(n, body):
        def one(i, carry):
            body(i)
            return carry
        lax.fori_loop(0, n, one, 0)

    def plane_peer(j):
        o = 10 + j
        o = jnp.where(o >= 16, o - 15, o)
        return lax.rem(x + o // 4, 4) * 4 + lax.rem(y + lax.rem(o, 4), 4)

    def ring_peer(j):
        half = (j + 1) // 2
        return lax.rem(row + 8 + jnp.where(lax.rem(j, 2) == 1, -half, half) + N_ROW, N_ROW)

    barrier = pltpu.get_barrier_semaphore()
    loop(15, lambda j: pl.semaphore_signal(barrier, inc=1, device_id=(ring_peer(j), col), device_id_type=MESH))
    loop(15, lambda j: pl.semaphore_signal(
        barrier, inc=1, device_id=(row, plane_peer(j) * 2 + core), device_id_type=MESH))
    pl.semaphore_signal(barrier, inc=1, device_id=twin, device_id_type=MESH)
    wide_r = lax.broadcasted_iota(jnp.int32, (768, 512), 0)
    wide_c = lax.broadcasted_iota(jnp.int32, (768, 512), 1)
    m[...] = jnp.where(wide_r == wide_c, 1.0, 0.0)
    a[...] = jnp.zeros((768, 768), jnp.float32)
    own_copy.wait()

    def first_piece(i):
        return first.at[pl.ds(pl.multiple_of(i * 8, 8), 8), :]

    holds_00 = (row == 0) & (col == 0)
    holds_10 = (row == 1) & (col == 0)
    holds_11 = (row == 1) & (col == 1)

    @pl.when(holds_00)
    def _():
        first[0:8, :] = own[0, 0:8, 0:SB]
        low[0, 0:8, :] = own[0, SB:SB + 8, :]

    @pl.when(holds_10)
    def _():
        low[0, 8:24, :] = own[0, 0:16, :]

    @pl.when(holds_11)
    def _():
        high[0] = own[0, 0:16, :]

    @pl.when(is_root)
    def _():
        panel[core] = own[...]

    @pl.when(row < 2)
    def _():
        top[row] = own[0]

    pl.semaphore_wait(barrier, 31)

    def own_rows(start, n):
        return own.at[0, pl.ds(pl.multiple_of(start, 8), n), :]

    @pl.when(holds_00)
    def _():
        loop(15, lambda j: send(
            own.at[0, pl.ds(pl.multiple_of(plane_peer(j) * 8, 8), 8), pl.ds(0, SB)], first_piece(plane_peer(j)),
            scatter_send.at[0], scatter_recv.at[0], (row, plane_peer(j) * 2)).start())
        loop(15, lambda j: send(
            own_rows(SB + plane_peer(j) * 8, 8), low.at[plane_peer(j), pl.ds(0, 8), :],
            scatter_send.at[1], scatter_recv.at[1], (row, plane_peer(j) * 2)).start())

    @pl.when(holds_10)
    def _():
        loop(15, lambda j: send(
            own_rows(plane_peer(j) * 16, 16), low.at[plane_peer(j), pl.ds(8, 16), :],
            scatter_send.at[2], scatter_recv.at[2], (row, plane_peer(j) * 2)).start())

    @pl.when(holds_11)
    def _():
        loop(15, lambda j: send(
            own_rows(plane_peer(j) * 16, 16), high.at[plane_peer(j)],
            scatter_send.at[3], scatter_recv.at[3], (row, plane_peer(j) * 2 + 1)).start())

    q = lax.rem(row, 2)
    delta = row - q
    top_depth = jnp.where(delta <= 8, delta, N_ROW - delta) // 2

    def top_to(offset):
        return (lax.rem(row + offset + N_ROW, N_ROW), col)

    def top_step(t):
        m = t - SKEW * top_depth
        slot = jnp.clip(m, 0, TOP_PARTS - 1)
        piece = top.at[q, pl.ds(pl.multiple_of(slot * 32, 32), 32), :]

        def go(kind, offset):
            send(piece, piece, top_send.at[kind], top_recv.at[q, slot], top_to(offset)).start()

        @pl.when((m >= 0) & (m < TOP_PARTS))
        def _():
            @pl.when(delta > 0)
            def _():
                send(piece, piece, top_send.at[0], top_recv.at[q, slot], here).wait_recv()

            @pl.when(delta < 8)
            def _():
                go(0, 2)

            @pl.when((delta == 0) | (delta >= 12))
            def _():
                go(1, -2)

            @pl.when((delta >= 2) & (delta <= 8))
            def _():
                go(2, -1)

            @pl.when(delta >= 8)
            def _():
                go(3, 1)

    def hops(p):
        return jnp.where(p == 0, 0, jnp.where(p == 2, 2, 1))

    def tree_step(t):
        for h in range(2):
            u, v = (x, y) if h == 0 else (y, x)
            p = jnp.where(v == 0, u, v)
            late = (u == 0) & (v != 0)

            def at(u2, v2):
                x2, y2 = (u2, v2) if h == 0 else (v2, u2)
                return (row, x2 * 8 + y2 * 2 + core)

            m = t - SKEW * (jnp.where(late, 2, hops(u)) + hops(v))
            slot = jnp.clip(m, 0, TREE_PARTS - 1)
            start = 128 * h + 64 * lax.rem(slot, 2)
            part = panel.at[core, slot // 2, pl.ds(pl.multiple_of(start, 64), 64), :]
            half0 = panel.at[core, slot // 2, pl.ds(pl.multiple_of(start, 32), 32), :]
            half1 = panel.at[core, slot // 2, pl.ds(pl.multiple_of(start + 32, 32), 32), :]

            def go(piece, kind, half, device):
                send(piece, piece, tree_send.at[h, kind], tree_recv.at[h, slot, half], device).start()

            @pl.when((m >= 0) & (m < TREE_PARTS))
            def _():
                @pl.when(((p == 1) | (p == 3)) & jnp.logical_not(late))
                def _():
                    send(part, part, tree_send.at[h, 0], tree_recv.at[h, slot, 0], here).wait_recv()

                @pl.when((p == 2) | late)
                def _():
                    send(half0, half0, tree_send.at[h, 0], tree_recv.at[h, slot, 0], here).wait_recv()
                    send(half1, half1, tree_send.at[h, 0], tree_recv.at[h, slot, 1], here).wait_recv()

                @pl.when((v == 0) & (u == 0))
                def _():
                    go(part, 0, 0, at(1, 0))
                    go(part, 1, 0, at(3, 0))

                @pl.when((p == 1) & jnp.logical_not(late))
                def _():
                    go(half0, 2, 0, at(jnp.where(v == 0, 2, u), jnp.where(v == 0, 0, 2)))

                @pl.when((p == 3) & jnp.logical_not(late))
                def _():
                    go(half1, 2, 1, at(jnp.where(v == 0, 2, u), jnp.where(v == 0, 0, 2)))

                @pl.when((v == 0) & (u != 0))
                def _():
                    go(part, 3, 0, at(u, 1))
                    go(part, 4, 0, at(u, 3))

                @pl.when((v != 0) & (u == 1))
                def _():
                    go(half0, 5, 0, at(0, v))

                @pl.when((v != 0) & (u == 3))
                def _():
                    go(half1, 5, 1, at(0, v))

                send(part, part, pair_send.at[h], pair_recv.at[h], twin).start()

    def tick(t):
        top_step(t)
        tree_step(t)

    def ticks(start, stop):
        def one(t, carry):
            tick(t)
            return carry
        lax.fori_loop(start, stop, one, 0)

    pieces = (
        (first_piece(chip), 0, 0),
        (low.at[chip, pl.ds(0, 8), :], 0, 0),
        (low.at[chip, pl.ds(8, 16), :], 1, 0),
        (high.at[chip], 1, 1),
    )
    def scattered(n):
        piece, start, carrier = pieces[n]

        @pl.when((row == start) & (core == carrier) & (chip != 0))
        def _():
            send(piece, piece, scatter_send.at[n], scatter_recv.at[n], here).wait_recv()

    def along_ring(n):
        piece, start, carrier = pieces[n]

        @pl.when((row == start) & (core == carrier))
        def _():
            loop(15, lambda j: send(piece, piece, ring_send.at[n], ring_recv.at[n], (ring_peer(j), col)).start())

    def ring_arrived(n):
        piece, start, _ = pieces[n]

        @pl.when(row != start)
        def _():
            send(piece, piece, ring_send.at[n], ring_recv.at[n], here).wait_recv()

    scattered(0)

    @pl.when(core == 0)
    def _():
        ring_arrived(0)
        loop(15, lambda j: send(
            first_piece(chip), first_piece(chip), plane_send.at[0], plane_recv.at[0],
            (row, plane_peer(j) * 2)).start())

    along_ring(0)
    for n in range(1, 4):
        scattered(n)
        along_ring(n)
    ticks(0, 6)

    @pl.when(core == 0)
    def _():
        ring_arrived(1)
        ring_arrived(2)
        loop(15, lambda j: send(
            low.at[chip], low.at[chip], plane_send.at[1], plane_recv.at[1], (row, plane_peer(j) * 2)).start())

    @pl.when(core == 1)
    def _():
        ring_arrived(3)
        loop(15, lambda j: send(
            high.at[chip], high.at[chip], plane_send.at[2], plane_recv.at[2],
            (row, plane_peer(j) * 2 + 1)).start())

    ticks(6, EARLY)

    @pl.when(core == 0)
    def _():
        send(first.at[pl.ds(0, 120), :], first.at[pl.ds(0, 120), :], plane_send.at[0], plane_recv.at[0], here).wait_recv()
        send(first, first, twin_send.at[0], twin_recv.at[0], twin).start()

    @pl.when(core == 1)
    def _():
        send(first, first, twin_send.at[0], twin_recv.at[0], here).wait_recv()

    def rest_in_plane():
        @pl.when(core == 0)
        def _():
            send(low.at[pl.ds(0, 15)], low.at[pl.ds(0, 15)], plane_send.at[1], plane_recv.at[1], here).wait_recv()
            send(low, low, twin_send.at[1], twin_recv.at[1], twin).start()

        @pl.when(core == 1)
        def _():
            send(high.at[pl.ds(0, 15)], high.at[pl.ds(0, 15)], plane_send.at[2], plane_recv.at[2], here).wait_recv()
            send(high, high, twin_send.at[2], twin_recv.at[2], twin).start()

    def rest_from_twin():
        @pl.when(core == 1)
        def _():
            send(low, low, twin_send.at[1], twin_recv.at[1], here).wait_recv()

        @pl.when(core == 0)
        def _():
            send(high, high, twin_send.at[2], twin_recv.at[2], here).wait_recv()

        for i in range(16):
            a[SB + 8 * i:SB + 8 * i + 8, 0:NB] = low[i, 0:8, :]
            a[NB + 16 * i:NB + 16 * i + 16, 0:NB] = low[i, 8:24, :]
            a[NB + 16 * i:NB + 16 * i + 16, NB:2 * NB] = high[i]

    a[0:SB, 0:SB] = first[...]

    def hook(s, k):
        if k % 3 == 2:
            if k == 8:
                pl.when(s == 0)(rest_in_plane)
            tick(EARLY + 6 * s + k // 3)

    def unpack(s):
        pl.when(s == 0)(rest_from_twin)
        tick(EARLY + 6 * s + 5)

    factor(a, m, z, lb, xs, hook, unpack)

    def top_arrived(m):
        piece = top.at[1 - q, pl.ds(pl.multiple_of(m * 32, 32), 32), :]
        send(piece, piece, top_send.at[0], top_recv.at[1 - q, m], here).wait_recv()

    @pl.when((row != 0) | (q != 1))
    def _():
        loop(TOP_PARTS, top_arrived)

    sq_r = lax.broadcasted_iota(jnp.int32, (NB, NB), 0)
    sq_c = lax.broadcasted_iota(jnp.int32, (NB, NB), 1)
    pick = jnp.where(sq_r == sq_c, -1.0, 0.0)
    upper = dot(z[0:NB, 0:NB], top[0])
    under = dot(z[NB:2 * NB, 0:NB], top[0]) + dot(z[NB:2 * NB, NB:2 * NB], top[1])
    upper = jnp.where(is_root, jnp.where(col == 0, pick, 0.0), upper)
    under = jnp.where(is_root, jnp.where(col == 1, pick, 0.0), under)
    w_hi[0:NB], w_lo[0:NB] = halves(dot_tn(z[0:NB, 0:NB], upper) + dot_tn(z[NB:2 * NB, 0:NB], under))
    w_hi[NB:2 * NB], w_lo[NB:2 * NB] = halves(dot_tn(z[NB:2 * NB, NB:2 * NB], under))

    for h in range(2):
        part = panel.at[1 - core, :, pl.ds(128 * h, 128), :]
        send(part, part, pair_send.at[h], pair_recv.at[h], here).wait_recv()

    for g in range(6):
        index = g * N_ROW + row
        value = jnp.where(is_root, 0.0, own[g])
        for k in range(2):
            hi, lo = halves(panel[k, g])
            w1, w2 = w_hi[NB * k:NB * k + NB], w_lo[NB * k:NB * k + NB]
            value = value - (dot16(hi, w1) + (dot16(hi, w2) + dot16(lo, w1)))
        keep = (index > col) | ((index == col) & ((sq_r >= sq_c) | jnp.logical_not(is_root)))
        o_ref[g] = jnp.where(keep, value, 0.0)

    def sent(ref, sem):
        send(ref, ref, sem, own_sem, here).wait_send()

    for n, holds, ref in (
        (0, holds_00, first.at[pl.ds(0, 120), :]),
        (1, holds_00, low.at[pl.ds(0, 15), pl.ds(0, 8), :]),
        (2, holds_10, low.at[pl.ds(0, 15), pl.ds(8, 16), :]),
        (3, holds_11, high.at[pl.ds(0, 15)]),
    ):
        pl.when(holds)(lambda n=n, ref=ref: sent(ref, scatter_send.at[n]))
        pl.when((row == pieces[n][1]) & (core == pieces[n][2]))(lambda n=n, ref=ref: sent(ref, ring_send.at[n]))

    @pl.when(core == 0)
    def _():
        sent(first.at[pl.ds(0, 120), :], plane_send.at[0])
        sent(low.at[pl.ds(0, 15)], plane_send.at[1])
        sent(first, twin_send.at[0])
        sent(low, twin_send.at[1])

    @pl.when(core == 1)
    def _():
        sent(high.at[pl.ds(0, 15)], plane_send.at[2])
        sent(high, twin_send.at[2])

    pl.when(delta < 8)(lambda: sent(top.at[0], top_send.at[0]))
    pl.when((delta == 0) | (delta >= 12))(lambda: sent(top.at[0], top_send.at[1]))
    pl.when((delta >= 2) & (delta <= 8))(lambda: sent(top.at[0], top_send.at[2]))
    pl.when(delta >= 8)(lambda: sent(top.at[0], top_send.at[3]))

    for h in range(2):
        u, v = (x, y) if h == 0 else (y, x)
        p = jnp.where(v == 0, u, v)
        whole = panel.at[core, :, pl.ds(0, 128), :]
        half = panel.at[core, :, pl.ds(0, 64), :]

        @pl.when((v == 0) & (u == 0))
        def _():
            sent(whole, tree_send.at[h, 0])
            sent(whole, tree_send.at[h, 1])

        pl.when(((p == 1) | (p == 3)) & ((v == 0) | (u != 0)))(lambda: sent(half, tree_send.at[h, 2]))
        pl.when((v != 0) & ((u == 1) | (u == 3)))(lambda: sent(half, tree_send.at[h, 5]))

        @pl.when((v == 0) & (u != 0))
        def _():
            sent(whole, tree_send.at[h, 3])
            sent(whole, tree_send.at[h, 4])

        sent(whole, pair_send.at[h])


def on_device(slab):
    dma = pltpu.SemaphoreType.DMA
    return pl.pallas_call(
        kernel,
        out_shape=jax.ShapeDtypeStruct(slab.shape, jnp.float32),
        in_specs=[pl.BlockSpec(memory_space=pl.ANY)],
        out_specs=pl.BlockSpec(memory_space=pltpu.VMEM),
        scratch_shapes=[
            pltpu.VMEM((6, NB, NB), jnp.float32),
            pltpu.VMEM((SB, SB), jnp.float32),
            pltpu.VMEM((16, 24, NB), jnp.float32),
            pltpu.VMEM((16, 16, NB), jnp.float32),
            pltpu.VMEM((2, NB, NB), jnp.float32),
            pltpu.VMEM((2, 6, NB, NB), jnp.float32),
            pltpu.VMEM((768, 768), jnp.float32),
            pltpu.VMEM((768, 512), jnp.float32),
            pltpu.VMEM((512, 512), jnp.float32),
            pltpu.VMEM((3, SB, SB), jnp.float32),
            pltpu.VMEM((SB, SB), jnp.float32),
            pltpu.VMEM((512, NB), jnp.bfloat16),
            pltpu.VMEM((512, NB), jnp.bfloat16),
            dma, dma((4,)), dma((4,)), dma((4,)), dma((4,)), dma((3,)), dma((3,)), dma((3,)), dma((3,)),
            dma((4,)), dma((2, TOP_PARTS)), dma((2, 6)), dma((2, TREE_PARTS, 2)), dma((2,)), dma((2,)),
        ],
        compiler_params=pltpu.CompilerParams(
            collective_id=0, has_side_effects=True, vmem_limit_bytes=VMEM
        ),
    )(slab)


def solution(mesh):
    spec = P(None, "row", "col")
    return jax.shard_map(on_device, mesh=mesh, in_specs=(spec,), out_specs=spec, check_vma=False)
```

```python
import jax
import jax.numpy as jnp
from jax import lax
from jax.experimental import pallas as pl
from jax.experimental.pallas import tpu as pltpu
from jax.sharding import PartitionSpec as P

HI = lax.Precision.HIGHEST
SB = 128


def contract(a, b, da, db):
    return lax.dot_general(a, b, (((da,), (db,)), ((), ())), precision=HI, preferred_element_type=jnp.float32)


def dot(a, b):
    return contract(a, b, 1, 0)


def dot_nt(a, b):
    return contract(a, b, 1, 1)


def dot_tn(a, b):
    return contract(a, b, 0, 0)


def lanes(part):
    return jnp.broadcast_to(part, (8, SB))


def eliminate(strips, after):
    sub = lax.broadcasted_iota(jnp.int32, (8, SB), 0)
    lane = lax.broadcasted_iota(jnp.int32, (8, SB), 1)
    strips = list(strips)
    scales = []
    for k in range(16):
        cur = strips[k]
        col = [lanes(cur[:, 8 * k + j:8 * k + j + 1]) for j in range(8)]
        scale = jnp.zeros((8, SB), jnp.float32)
        pairs = []
        for j in range(0, 8, 2):
            a = lanes(col[j][j:j + 1])
            b = lanes(col[j][j + 1:j + 2])
            c = lanes(col[j + 1][j + 1:j + 2])
            det = a * c - b * b
            inv = 1.0 / det
            over_a = 1.0 / a
            scale = jnp.where(sub == j, lax.rsqrt(a), jnp.where(sub == j + 1, lax.rsqrt(det * over_a), scale))
            low0 = jnp.where(sub > j + 1, col[j], 0.0)
            low1 = jnp.where(sub > j + 1, col[j + 1], 0.0)

            def solve(r0, r1):
                return (c * r0 - b * r1) * inv, (a * r1 - b * r0) * inv

            ratios = []
            for i in range(j + 2, 8):
                u, w = solve(lanes(col[i][j:j + 1]), lanes(col[i][j + 1:j + 2]))
                col[i] = col[i] - low0 * u - low1 * w
                ratios.append((u, w))
            r0 = jnp.where(lane == 8 * k + j, a + 1.0, lanes(cur[j:j + 1]))
            r1 = jnp.where(lane == 8 * k + j + 1, c + 1.0, lanes(cur[j + 1:j + 2]))
            u, w = solve(r0, r1)
            cur = cur - low0 * u - low1 * w - jnp.where(sub == j + 1, b * over_a, 0.0) * r0
            pairs.append((ratios, u, w))
        strips[k] = cur
        scales.append(scale)
        for t in range(k + 1, 16):
            acc = strips[t]
            c = [lanes(acc[:, 8 * k + j:8 * k + j + 1]) for j in range(8)]
            for p, (ratios, u, w) in enumerate(pairs):
                c0, c1 = c[2 * p], c[2 * p + 1]
                for i, (ui, wi) in enumerate(ratios):
                    c[2 * p + 2 + i] = c[2 * p + 2 + i] - c0 * ui - c1 * wi
                acc = acc - c0 * u - c1 * w
            strips[t] = acc
        after(k)
    return strips, scales


def block(i):
    return pl.ds(pl.multiple_of(i * SB, SB), SB)


def factor(a, m, z, lb, xs, hook, unpack):
    sub = lax.broadcasted_iota(jnp.int32, (8, SB), 0)
    lane = lax.broadcasted_iota(jnp.int32, (8, SB), 1)
    xs[...] = jnp.zeros((SB, SB), jnp.float32)
    lb[...] = jnp.zeros((3, SB, SB), jnp.float32)

    def step(s, carry):
        p = jnp.maximum(s - 1, 0)

        def lower(i):
            lb[i] = dot_nt(a[block(s + i), block(p)], xs[...])

        def schur(i, j):
            a[block(s + i), block(s + j)] = a[block(s + i), block(s + j)] - dot_nt(lb[i], lb[j])

        def rows():
            z[block(p), :] = dot(xs[...], m[block(p), :])

        def spread(i):
            m[block(s + i), :] = m[block(s + i), :] - dot(lb[i], z[block(p), :])

        jobs = {
            0: (lambda: lower(1), lambda: lower(2)),
            1: (rows,),
            3: (lambda: schur(1, 0), lambda: schur(1, 1)),
            4: (lambda: schur(2, 0), lambda: schur(2, 1)),
            5: (lambda: schur(2, 2),),
            6: (lambda: spread(0),),
            9: (lambda: spread(1),),
            12: (lambda: spread(2),),
        }

        def after(k):
            for job in jobs.get(k, ()):
                job()
            hook(s, k)

        strips, scales = eliminate([a[pl.ds(pl.multiple_of(s * SB + 8 * t, 8), 8), block(s)] for t in range(16)], after)
        unpack(s)
        for t in range(16):
            diag = sub + 8 * t
            xs[8 * t:8 * t + 8, :] = jnp.where(
                lane < diag, strips[t] * scales[t], jnp.where(lane == diag, scales[t], 0.0))

        @pl.when(s < 3)
        def _():
            lb[0] = dot_nt(a[block(s + 1), block(s)], xs[...])
            a[block(s + 1), block(s + 1)] = a[block(s + 1), block(s + 1)] - dot_nt(lb[0], lb[0])
        return carry

    lax.fori_loop(0, 4, step, 0)
    z[block(3), :] = dot(xs[...], m[block(3), :])

NB = 256
N_ROW = 16
N_COL = 32
MESH = pl.DeviceIdType.MESH
TREE_PARTS = 6
TOP_PARTS = 4
SKEW = 3
TOP_LAG = 2
FAR_TICKS = 3
NEAR_TICKS = 3
MID_TICKS = 4
EARLY = 6
TICKS = (4, 9, 14)
TREE_ROWS = 768 // TREE_PARTS
TOP_ROWS = NB // TOP_PARTS
VMEM = 28 * 2**20


def halves(v):
    hi = v.astype(jnp.bfloat16)
    return hi, (v - hi.astype(jnp.float32)).astype(jnp.bfloat16)


def dot16(p, q):
    return lax.dot_general(p, q, (((1,), (0,)), ((), ())), preferred_element_type=jnp.float32)


def send(src, dst, send_sem, recv_sem, device):
    return pltpu.make_async_remote_copy(
        src_ref=src, dst_ref=dst, send_sem=send_sem, recv_sem=recv_sem, device_id=device, device_id_type=MESH
    )


def kernel(
    x_ref, o_ref, own, first, low, high, top, panel, a, m, z, lb, xs, w_hi, w_lo,
    own_sem, scatter_send, scatter_recv, ring_send, ring_recv, plane_send, plane_recv, twin_send, twin_recv,
    top_send, top_recv, tree_send, tree_recv, pair_send, pair_recv,
):
    row = lax.axis_index("row")
    col = lax.axis_index("col")
    core = lax.rem(col, 2)
    chip = col // 2
    x = chip // 4
    y = lax.rem(chip, 4)
    is_root = col < 2
    twin = (row, col + 1 - 2 * core)
    here = (row, col)

    own_copy = pltpu.make_async_copy(x_ref, own, own_sem)
    own_copy.start()

    def loop(n, body):
        def one(i, carry):
            body(i)
            return carry
        lax.fori_loop(0, n, one, 0)

    def plane_peer(j):
        o = 10 + j
        o = jnp.where(o >= 16, o - 15, o)
        return lax.rem(x + o // 4, 4) * 4 + lax.rem(y + lax.rem(o, 4), 4)

    def ring_peer(j):
        half = (j + 1) // 2
        return lax.rem(row + 8 + jnp.where(lax.rem(j, 2) == 1, -half, half) + N_ROW, N_ROW)

    barrier = pltpu.get_barrier_semaphore()
    loop(15, lambda j: pl.semaphore_signal(barrier, inc=1, device_id=(ring_peer(j), col), device_id_type=MESH))
    loop(15, lambda j: pl.semaphore_signal(
        barrier, inc=1, device_id=(row, plane_peer(j) * 2 + core), device_id_type=MESH))
    pl.semaphore_signal(barrier, inc=1, device_id=twin, device_id_type=MESH)
    wide_r = lax.broadcasted_iota(jnp.int32, (768, 512), 0)
    wide_c = lax.broadcasted_iota(jnp.int32, (768, 512), 1)
    m[...] = jnp.where(wide_r == wide_c, 1.0, 0.0)
    a[...] = jnp.zeros((768, 768), jnp.float32)
    own_copy.wait()

    def first_piece(i):
        return first.at[pl.ds(pl.multiple_of(i * 8, 8), 8), :]

    holds_00 = (row == 0) & (col == 0)
    holds_10 = (row == 1) & (col == 0)
    holds_11 = (row == 1) & (col == 1)

    @pl.when(holds_00)
    def _():
        first[0:8, :] = own[0, 0:8, 0:SB]
        low[0, 0:8, :] = own[0, SB:SB + 8, :]

    @pl.when(holds_10)
    def _():
        low[0, 8:24, :] = own[0, 0:16, :]

    @pl.when(holds_11)
    def _():
        high[0] = own[0, 0:16, :]

    @pl.when(is_root)
    def _():
        panel[core] = own[...]

    @pl.when(row < 2)
    def _():
        top[row] = own[0]

    pl.semaphore_wait(barrier, 31)

    def own_rows(start, n):
        return own.at[0, pl.ds(pl.multiple_of(start, 8), n), :]

    @pl.when(holds_00)
    def _():
        loop(15, lambda j: send(
            own.at[0, pl.ds(pl.multiple_of(plane_peer(j) * 8, 8), 8), pl.ds(0, SB)], first_piece(plane_peer(j)),
            scatter_send.at[0], scatter_recv.at[0], (row, plane_peer(j) * 2)).start())
        loop(15, lambda j: send(
            own_rows(SB + plane_peer(j) * 8, 8), low.at[plane_peer(j), pl.ds(0, 8), :],
            scatter_send.at[1], scatter_recv.at[1], (row, plane_peer(j) * 2)).start())

    @pl.when(holds_10)
    def _():
        loop(15, lambda j: send(
            own_rows(plane_peer(j) * 16, 16), low.at[plane_peer(j), pl.ds(8, 16), :],
            scatter_send.at[2], scatter_recv.at[2], (row, plane_peer(j) * 2)).start())

    @pl.when(holds_11)
    def _():
        loop(15, lambda j: send(
            own_rows(plane_peer(j) * 16, 16), high.at[plane_peer(j)],
            scatter_send.at[3], scatter_recv.at[3], (row, plane_peer(j) * 2 + 1)).start())

    q = lax.rem(row, 2)
    delta = row - q
    top_depth = jnp.where(delta <= 8, delta, N_ROW - delta) // 2

    top_goes = (
        delta < 8,
        (delta == 0) | (delta >= 12),
        (delta >= 2) & (delta <= 8),
        delta >= 8,
    )

    def top_to(offset):
        return (lax.rem(row + offset + N_ROW, N_ROW), col)

    def top_step(t):
        m = t - jnp.where(delta == 0, 0, TOP_LAG + SKEW * top_depth)
        slot = jnp.clip(m, 0, TOP_PARTS - 1)
        piece = top.at[q, pl.ds(pl.multiple_of(slot * TOP_ROWS, TOP_ROWS), TOP_ROWS), :]

        def go(kind, offset):
            send(piece, piece, top_send.at[kind], top_recv.at[q, slot], top_to(offset)).start()

        @pl.when((m >= 0) & (m < TOP_PARTS))
        def _():
            @pl.when(delta > 0)
            def _():
                send(piece, piece, top_send.at[0], top_recv.at[q, slot], here).wait_recv()

            for kind, offset in enumerate((2, -2, -1, 1)):
                pl.when(top_goes[kind])(lambda kind=kind, offset=offset: go(kind, offset))

    def hops(p):
        return jnp.where(p == 0, 0, jnp.where(p == 2, 2, 1))

    def tree_step(t):
        for h in range(2):
            u, v = (x, y) if h == 0 else (y, x)
            p = jnp.where(v == 0, u, v)
            late = (u == 0) & (v != 0)

            def at(u2, v2):
                x2, y2 = (u2, v2) if h == 0 else (v2, u2)
                return (row, x2 * 8 + y2 * 2 + core)

            m = t - SKEW * (jnp.where(late, 2, hops(u)) + hops(v))
            slot = jnp.clip(m, 0, TREE_PARTS - 1)
            start = 128 * h + TREE_ROWS * lax.rem(slot, TREE_PARTS // 6)
            part = panel.at[core, slot // (TREE_PARTS // 6), pl.ds(pl.multiple_of(start, TREE_ROWS), TREE_ROWS), :]
            half0 = panel.at[core, slot // (TREE_PARTS // 6), pl.ds(pl.multiple_of(start, TREE_ROWS // 2), TREE_ROWS // 2), :]
            half1 = panel.at[core, slot // (TREE_PARTS // 6), pl.ds(pl.multiple_of(start + TREE_ROWS // 2, TREE_ROWS // 2), TREE_ROWS // 2), :]

            def go(piece, kind, half, device):
                send(piece, piece, tree_send.at[h, kind], tree_recv.at[h, slot, half], device).start()

            @pl.when((m >= 0) & (m < TREE_PARTS))
            def _():
                @pl.when(((p == 1) | (p == 3)) & jnp.logical_not(late))
                def _():
                    send(part, part, tree_send.at[h, 0], tree_recv.at[h, slot, 0], here).wait_recv()

                @pl.when((p == 2) | late)
                def _():
                    send(half0, half0, tree_send.at[h, 0], tree_recv.at[h, slot, 0], here).wait_recv()
                    send(half1, half1, tree_send.at[h, 0], tree_recv.at[h, slot, 1], here).wait_recv()

                @pl.when((v == 0) & (u == 0))
                def _():
                    go(part, 0, 0, at(1, 0))
                    go(part, 1, 0, at(3, 0))

                @pl.when((p == 1) & jnp.logical_not(late))
                def _():
                    go(half0, 2, 0, at(jnp.where(v == 0, 2, u), jnp.where(v == 0, 0, 2)))

                @pl.when((p == 3) & jnp.logical_not(late))
                def _():
                    go(half1, 2, 1, at(jnp.where(v == 0, 2, u), jnp.where(v == 0, 0, 2)))

                @pl.when((v == 0) & (u != 0))
                def _():
                    go(part, 3, 0, at(u, 1))
                    go(part, 4, 0, at(u, 3))

                @pl.when((v != 0) & (u == 1))
                def _():
                    go(half0, 5, 0, at(0, v))

                @pl.when((v != 0) & (u == 3))
                def _():
                    go(half1, 5, 1, at(0, v))

                send(part, part, pair_send.at[h], pair_recv.at[h], twin).start()

    def tick(t):
        top_step(t)
        tree_step(t)

    def ticks(start, stop):
        def one(t, carry):
            tick(t)
            return carry
        lax.fori_loop(start, stop, one, 0)

    pieces = (
        (first_piece(chip), 0, 0),
        (low.at[chip, pl.ds(0, 8), :], 0, 0),
        (low.at[chip, pl.ds(8, 16), :], 1, 0),
        (high.at[chip], 1, 1),
    )
    def scattered(n):
        piece, start, carrier = pieces[n]

        @pl.when((row == start) & (core == carrier) & (chip != 0))
        def _():
            send(piece, piece, scatter_send.at[n], scatter_recv.at[n], here).wait_recv()

    def along_ring(n):
        piece, start, carrier = pieces[n]

        @pl.when((row == start) & (core == carrier))
        def _():
            loop(15, lambda j: send(piece, piece, ring_send.at[n], ring_recv.at[n], (ring_peer(j), col)).start())

    def ring_arrived(n):
        piece, start, _ = pieces[n]

        @pl.when(row != start)
        def _():
            send(piece, piece, ring_send.at[n], ring_recv.at[n], here).wait_recv()

    def gather_first():
        loop(15, lambda j: send(
            first_piece(chip), first_piece(chip), plane_send.at[0], plane_recv.at[0],
            (row, plane_peer(j) * 2)).start())

    pl.when(row >= 2)(lambda: ticks(0, FAR_TICKS))
    scattered(0)
    pl.when((row == 0) & (core == 0))(gather_first)
    for n in range(4):
        if n:
            scattered(n)
        along_ring(n)
    pl.when(row < 2)(lambda: ticks(0, NEAR_TICKS))

    @pl.when((row != 0) & (core == 0))
    def _():
        ring_arrived(0)
        gather_first()

    pl.when(row < 2)(lambda: ticks(NEAR_TICKS, FAR_TICKS))
    ticks(FAR_TICKS, MID_TICKS)

    @pl.when(core == 0)
    def _():
        ring_arrived(1)
        ring_arrived(2)
        loop(15, lambda j: send(
            low.at[chip], low.at[chip], plane_send.at[1], plane_recv.at[1], (row, plane_peer(j) * 2)).start())

    @pl.when(core == 1)
    def _():
        ring_arrived(3)
        loop(15, lambda j: send(
            high.at[chip], high.at[chip], plane_send.at[2], plane_recv.at[2],
            (row, plane_peer(j) * 2 + 1)).start())

    ticks(MID_TICKS, EARLY)

    @pl.when(core == 0)
    def _():
        send(first.at[pl.ds(0, 120), :], first.at[pl.ds(0, 120), :], plane_send.at[0], plane_recv.at[0], here).wait_recv()
        send(first, first, twin_send.at[0], twin_recv.at[0], twin).start()

    @pl.when(core == 1)
    def _():
        send(first, first, twin_send.at[0], twin_recv.at[0], here).wait_recv()

    def rest_in_plane():
        @pl.when(core == 0)
        def _():
            send(low.at[pl.ds(0, 15)], low.at[pl.ds(0, 15)], plane_send.at[1], plane_recv.at[1], here).wait_recv()
            send(low, low, twin_send.at[1], twin_recv.at[1], twin).start()

        @pl.when(core == 1)
        def _():
            send(high.at[pl.ds(0, 15)], high.at[pl.ds(0, 15)], plane_send.at[2], plane_recv.at[2], here).wait_recv()
            send(high, high, twin_send.at[2], twin_recv.at[2], twin).start()

    def rest_from_twin():
        @pl.when(core == 1)
        def _():
            send(low, low, twin_send.at[1], twin_recv.at[1], here).wait_recv()

        @pl.when(core == 0)
        def _():
            send(high, high, twin_send.at[2], twin_recv.at[2], here).wait_recv()

        for i in range(16):
            a[SB + 8 * i:SB + 8 * i + 8, 0:NB] = low[i, 0:8, :]
            a[NB + 16 * i:NB + 16 * i + 16, 0:NB] = low[i, 8:24, :]
            a[NB + 16 * i:NB + 16 * i + 16, NB:2 * NB] = high[i]

    a[0:SB, 0:SB] = first[...]

    def hook(s, k):
        if k == 7:
            pl.when(s == 0)(rest_in_plane)
        if k in TICKS:
            tick(EARLY + len(TICKS) * s + TICKS.index(k))

    def unpack(s):
        pl.when(s == 0)(rest_from_twin)

    factor(a, m, z, lb, xs, hook, unpack)

    def top_arrived(m):
        piece = top.at[1 - q, pl.ds(pl.multiple_of(m * TOP_ROWS, TOP_ROWS), TOP_ROWS), :]
        send(piece, piece, top_send.at[0], top_recv.at[1 - q, m], here).wait_recv()

    @pl.when((row != 0) | (q != 1))
    def _():
        loop(TOP_PARTS, top_arrived)

    sq_r = lax.broadcasted_iota(jnp.int32, (NB, NB), 0)
    sq_c = lax.broadcasted_iota(jnp.int32, (NB, NB), 1)
    pick = jnp.where(sq_r == sq_c, -1.0, 0.0)
    upper = dot(z[0:NB, 0:NB], top[0])
    under = dot(z[NB:2 * NB, 0:NB], top[0]) + dot(z[NB:2 * NB, NB:2 * NB], top[1])
    upper = jnp.where(is_root, jnp.where(col == 0, pick, 0.0), upper)
    under = jnp.where(is_root, jnp.where(col == 1, pick, 0.0), under)
    w_hi[0:NB], w_lo[0:NB] = halves(dot_tn(z[0:NB, 0:NB], upper) + dot_tn(z[NB:2 * NB, 0:NB], under))
    w_hi[NB:2 * NB], w_lo[NB:2 * NB] = halves(dot_tn(z[NB:2 * NB, NB:2 * NB], under))

    for h in range(2):
        part = panel.at[1 - core, :, pl.ds(128 * h, 128), :]
        send(part, part, pair_send.at[h], pair_recv.at[h], here).wait_recv()

    for g in range(6):
        index = g * N_ROW + row
        value = jnp.where(is_root, 0.0, own[g])
        for k in range(2):
            hi, lo = halves(panel[k, g])
            w1, w2 = w_hi[NB * k:NB * k + NB], w_lo[NB * k:NB * k + NB]
            value = value - (dot16(hi, w1) + (dot16(hi, w2) + dot16(lo, w1)))
        keep = (index > col) | ((index == col) & ((sq_r >= sq_c) | jnp.logical_not(is_root)))
        o_ref[g] = jnp.where(keep, value, 0.0)

    def sent(ref, sem):
        send(ref, ref, sem, own_sem, here).wait_send()

    for n, holds, ref in (
        (0, holds_00, first.at[pl.ds(0, 120), :]),
        (1, holds_00, low.at[pl.ds(0, 15), pl.ds(0, 8), :]),
        (2, holds_10, low.at[pl.ds(0, 15), pl.ds(8, 16), :]),
        (3, holds_11, high.at[pl.ds(0, 15)]),
    ):
        pl.when(holds)(lambda n=n, ref=ref: sent(ref, scatter_send.at[n]))
        pl.when((row == pieces[n][1]) & (core == pieces[n][2]))(lambda n=n, ref=ref: sent(ref, ring_send.at[n]))

    @pl.when(core == 0)
    def _():
        sent(first.at[pl.ds(0, 120), :], plane_send.at[0])
        sent(low.at[pl.ds(0, 15)], plane_send.at[1])
        sent(first, twin_send.at[0])
        sent(low, twin_send.at[1])

    @pl.when(core == 1)
    def _():
        sent(high.at[pl.ds(0, 15)], plane_send.at[2])
        sent(high, twin_send.at[2])

    for kind in range(4):
        pl.when(top_goes[kind])(lambda kind=kind: sent(top.at[0], top_send.at[kind]))

    for h in range(2):
        u, v = (x, y) if h == 0 else (y, x)
        p = jnp.where(v == 0, u, v)
        whole = panel.at[core, :, pl.ds(0, 128), :]
        half = panel.at[core, :, pl.ds(0, 64), :]

        @pl.when((v == 0) & (u == 0))
        def _():
            sent(whole, tree_send.at[h, 0])
            sent(whole, tree_send.at[h, 1])

        pl.when(((p == 1) | (p == 3)) & ((v == 0) | (u != 0)))(lambda: sent(half, tree_send.at[h, 2]))
        pl.when((v != 0) & ((u == 1) | (u == 3)))(lambda: sent(half, tree_send.at[h, 5]))

        @pl.when((v == 0) & (u != 0))
        def _():
            sent(whole, tree_send.at[h, 3])
            sent(whole, tree_send.at[h, 4])

        sent(whole, pair_send.at[h])


def on_device(slab):
    dma = pltpu.SemaphoreType.DMA
    return pl.pallas_call(
        kernel,
        out_shape=jax.ShapeDtypeStruct(slab.shape, jnp.float32),
        in_specs=[pl.BlockSpec(memory_space=pl.ANY)],
        out_specs=pl.BlockSpec(memory_space=pltpu.VMEM),
        scratch_shapes=[
            pltpu.VMEM((6, NB, NB), jnp.float32),
            pltpu.VMEM((SB, SB), jnp.float32),
            pltpu.VMEM((16, 24, NB), jnp.float32),
            pltpu.VMEM((16, 16, NB), jnp.float32),
            pltpu.VMEM((2, NB, NB), jnp.float32),
            pltpu.VMEM((2, 6, NB, NB), jnp.float32),
            pltpu.VMEM((768, 768), jnp.float32),
            pltpu.VMEM((768, 512), jnp.float32),
            pltpu.VMEM((512, 512), jnp.float32),
            pltpu.VMEM((3, SB, SB), jnp.float32),
            pltpu.VMEM((SB, SB), jnp.float32),
            pltpu.VMEM((512, NB), jnp.bfloat16),
            pltpu.VMEM((512, NB), jnp.bfloat16),
            dma, dma((4,)), dma((4,)), dma((4,)), dma((4,)), dma((3,)), dma((3,)), dma((3,)), dma((3,)),
            dma((4,)), dma((2, TOP_PARTS)), dma((2, 6)), dma((2, TREE_PARTS, 2)), dma((2,)), dma((2,)),
        ],
        compiler_params=pltpu.CompilerParams(
            collective_id=0, has_side_effects=True, vmem_limit_bytes=VMEM
        ),
    )(slab)


def solution(mesh):
    spec = P(None, "row", "col")
    return jax.shard_map(on_device, mesh=mesh, in_specs=(spec,), out_specs=spec, check_vma=False)
```

```python
import jax
import jax.numpy as jnp
from jax import lax
from jax.experimental import pallas as pl
from jax.experimental.pallas import tpu as pltpu
from jax.sharding import PartitionSpec as P

HI = lax.Precision.HIGHEST
SB = 128


def contract(a, b, da, db):
    return lax.dot_general(a, b, (((da,), (db,)), ((), ())), precision=HI, preferred_element_type=jnp.float32)


def dot(a, b):
    return contract(a, b, 1, 0)


def dot_nt(a, b):
    return contract(a, b, 1, 1)


def dot_tn(a, b):
    return contract(a, b, 0, 0)


def lanes(part):
    return jnp.broadcast_to(part, (8, SB))


def eliminate(strips, after):
    sub = lax.broadcasted_iota(jnp.int32, (8, SB), 0)
    lane = lax.broadcasted_iota(jnp.int32, (8, SB), 1)
    strips = list(strips)
    scales = []
    for k in range(16):
        cur = strips[k]
        col = [lanes(cur[:, 8 * k + j:8 * k + j + 1]) for j in range(8)]
        scale = jnp.zeros((8, SB), jnp.float32)
        pairs = []
        for j in range(0, 8, 2):
            a = lanes(col[j][j:j + 1])
            b = lanes(col[j][j + 1:j + 2])
            c = lanes(col[j + 1][j + 1:j + 2])
            det = a * c - b * b
            inv = 1.0 / det
            over_a = 1.0 / a
            scale = jnp.where(sub == j, lax.rsqrt(a), jnp.where(sub == j + 1, lax.rsqrt(det * over_a), scale))
            low0 = jnp.where(sub > j + 1, col[j], 0.0)
            low1 = jnp.where(sub > j + 1, col[j + 1], 0.0)

            def solve(r0, r1):
                return (c * r0 - b * r1) * inv, (a * r1 - b * r0) * inv

            ratios = []
            for i in range(j + 2, 8):
                u, w = solve(lanes(col[i][j:j + 1]), lanes(col[i][j + 1:j + 2]))
                col[i] = col[i] - low0 * u - low1 * w
                ratios.append((u, w))
            r0 = jnp.where(lane == 8 * k + j, a + 1.0, lanes(cur[j:j + 1]))
            r1 = jnp.where(lane == 8 * k + j + 1, c + 1.0, lanes(cur[j + 1:j + 2]))
            u, w = solve(r0, r1)
            cur = cur - low0 * u - low1 * w - jnp.where(sub == j + 1, b * over_a, 0.0) * r0
            pairs.append((ratios, u, w))
        strips[k] = cur
        scales.append(scale)
        for t in range(k + 1, 16):
            acc = strips[t]
            c = [lanes(acc[:, 8 * k + j:8 * k + j + 1]) for j in range(8)]
            for p, (ratios, u, w) in enumerate(pairs):
                c0, c1 = c[2 * p], c[2 * p + 1]
                for i, (ui, wi) in enumerate(ratios):
                    c[2 * p + 2 + i] = c[2 * p + 2 + i] - c0 * ui - c1 * wi
                acc = acc - c0 * u - c1 * w
            strips[t] = acc
        after(k)
    return strips, scales


def block(i):
    return pl.ds(pl.multiple_of(i * SB, SB), SB)


def factor(a, m, z, lb, xs, hook, unpack):
    sub = lax.broadcasted_iota(jnp.int32, (8, SB), 0)
    lane = lax.broadcasted_iota(jnp.int32, (8, SB), 1)
    xs[...] = jnp.zeros((SB, SB), jnp.float32)
    lb[...] = jnp.zeros((3, SB, SB), jnp.float32)

    def step(s, carry):
        p = jnp.maximum(s - 1, 0)

        def lower(i):
            lb[i] = dot_nt(a[block(s + i), block(p)], xs[...])

        def schur(i, j):
            a[block(s + i), block(s + j)] = a[block(s + i), block(s + j)] - dot_nt(lb[i], lb[j])

        def rows():
            z[block(p), :] = dot(xs[...], m[block(p), :])

        def spread(i):
            m[block(s + i), :] = m[block(s + i), :] - dot(lb[i], z[block(p), :])

        jobs = {
            0: (lambda: lower(1), lambda: lower(2)),
            1: (rows,),
            3: (lambda: schur(1, 0), lambda: schur(1, 1)),
            4: (lambda: schur(2, 0), lambda: schur(2, 1)),
            5: (lambda: schur(2, 2),),
            6: (lambda: spread(0),),
            9: (lambda: spread(1),),
            12: (lambda: spread(2),),
        }

        def after(k):
            for job in jobs.get(k, ()):
                job()
            hook(s, k)

        strips, scales = eliminate([a[pl.ds(pl.multiple_of(s * SB + 8 * t, 8), 8), block(s)] for t in range(16)], after)
        unpack(s)
        for t in range(16):
            diag = sub + 8 * t
            xs[8 * t:8 * t + 8, :] = jnp.where(
                lane < diag, strips[t] * scales[t], jnp.where(lane == diag, scales[t], 0.0))

        @pl.when(s < 3)
        def _():
            lb[0] = dot_nt(a[block(s + 1), block(s)], xs[...])
            a[block(s + 1), block(s + 1)] = a[block(s + 1), block(s + 1)] - dot_nt(lb[0], lb[0])
        return carry

    lax.fori_loop(0, 4, step, 0)
    z[block(3), :] = dot(xs[...], m[block(3), :])

NB = 256
N_ROW = 16
N_COL = 32
MESH = pl.DeviceIdType.MESH
TREE_PARTS = 6
TOP_PARTS = 4
SKEW = 3
TOP_LAG = 2
FAR_TICKS = 3
NEAR_TICKS = 3
MID_TICKS = 4
EARLY = 6
TICKS = (4, 9, 14)
TREE_ROWS = 768 // TREE_PARTS
TOP_ROWS = NB // TOP_PARTS
VMEM = 28 * 2**20


def halves(v):
    hi = v.astype(jnp.bfloat16)
    return hi, (v - hi.astype(jnp.float32)).astype(jnp.bfloat16)


def dot16(p, q):
    return lax.dot_general(p, q, (((1,), (0,)), ((), ())), preferred_element_type=jnp.float32)


def dot3(p, q, dim):
    (p1, p2), (q1, q2) = halves(p), halves(q)

    def one(u, v):
        return lax.dot_general(u, v, (((dim,), (0,)), ((), ())), preferred_element_type=jnp.float32)

    return one(p1, q1) + (one(p1, q2) + one(p2, q1))


def send(src, dst, send_sem, recv_sem, device):
    return pltpu.make_async_remote_copy(
        src_ref=src, dst_ref=dst, send_sem=send_sem, recv_sem=recv_sem, device_id=device, device_id_type=MESH
    )


def kernel(
    x_ref, o_ref, own, first, low, high, top, panel, a, m, z, lb, xs, w_hi, w_lo,
    own_sem, scatter_send, scatter_recv, ring_send, ring_recv, plane_send, plane_recv, twin_send, twin_recv,
    top_send, top_recv, tree_send, tree_recv, pair_send, pair_recv,
):
    row = lax.axis_index("row")
    col = lax.axis_index("col")
    core = lax.rem(col, 2)
    chip = col // 2
    x = chip // 4
    y = lax.rem(chip, 4)
    is_root = col < 2
    twin = (row, col + 1 - 2 * core)
    here = (row, col)

    own_copy = pltpu.make_async_copy(x_ref, own, own_sem)
    own_copy.start()

    def loop(n, body):
        def one(i, carry):
            body(i)
            return carry
        lax.fori_loop(0, n, one, 0)

    def plane_peer(j):
        o = 10 + j
        o = jnp.where(o >= 16, o - 15, o)
        return lax.rem(x + o // 4, 4) * 4 + lax.rem(y + lax.rem(o, 4), 4)

    def ring_peer(j):
        half = (j + 1) // 2
        return lax.rem(row + 8 + jnp.where(lax.rem(j, 2) == 1, -half, half) + N_ROW, N_ROW)

    barrier = pltpu.get_barrier_semaphore()
    loop(15, lambda j: pl.semaphore_signal(barrier, inc=1, device_id=(ring_peer(j), col), device_id_type=MESH))
    loop(15, lambda j: pl.semaphore_signal(
        barrier, inc=1, device_id=(row, plane_peer(j) * 2 + core), device_id_type=MESH))
    pl.semaphore_signal(barrier, inc=1, device_id=twin, device_id_type=MESH)
    wide_r = lax.broadcasted_iota(jnp.int32, (768, 512), 0)
    wide_c = lax.broadcasted_iota(jnp.int32, (768, 512), 1)
    m[...] = jnp.where(wide_r == wide_c, 1.0, 0.0)
    a[...] = jnp.zeros((768, 768), jnp.float32)
    own_copy.wait()

    def first_piece(i):
        return first.at[pl.ds(pl.multiple_of(i * 8, 8), 8), :]

    holds_00 = (row == 0) & (col == 0)
    holds_10 = (row == 1) & (col == 0)
    holds_11 = (row == 1) & (col == 1)

    @pl.when(holds_00)
    def _():
        first[0:8, :] = own[0, 0:8, 0:SB]
        low[0, 0:8, :] = own[0, SB:SB + 8, :]

    @pl.when(holds_10)
    def _():
        low[0, 8:24, :] = own[0, 0:16, :]

    @pl.when(holds_11)
    def _():
        high[0] = own[0, 0:16, :]

    @pl.when(is_root)
    def _():
        panel[core] = own[...]

    @pl.when(row < 2)
    def _():
        top[row] = own[0]

    pl.semaphore_wait(barrier, 31)

    def own_rows(start, n):
        return own.at[0, pl.ds(pl.multiple_of(start, 8), n), :]

    @pl.when(holds_00)
    def _():
        loop(15, lambda j: send(
            own.at[0, pl.ds(pl.multiple_of(plane_peer(j) * 8, 8), 8), pl.ds(0, SB)], first_piece(plane_peer(j)),
            scatter_send.at[0], scatter_recv.at[0], (row, plane_peer(j) * 2)).start())
        loop(15, lambda j: send(
            own_rows(SB + plane_peer(j) * 8, 8), low.at[plane_peer(j), pl.ds(0, 8), :],
            scatter_send.at[1], scatter_recv.at[1], (row, plane_peer(j) * 2)).start())

    @pl.when(holds_10)
    def _():
        loop(15, lambda j: send(
            own_rows(plane_peer(j) * 16, 16), low.at[plane_peer(j), pl.ds(8, 16), :],
            scatter_send.at[2], scatter_recv.at[2], (row, plane_peer(j) * 2)).start())

    @pl.when(holds_11)
    def _():
        loop(15, lambda j: send(
            own_rows(plane_peer(j) * 16, 16), high.at[plane_peer(j)],
            scatter_send.at[3], scatter_recv.at[3], (row, plane_peer(j) * 2 + 1)).start())

    q = lax.rem(row, 2)
    delta = row - q
    top_depth = jnp.where(delta <= 8, delta, N_ROW - delta) // 2

    top_goes = (
        delta < 8,
        (delta == 0) | (delta >= 12),
        (delta >= 2) & (delta <= 8),
        delta >= 8,
    )

    def top_to(offset):
        return (lax.rem(row + offset + N_ROW, N_ROW), col)

    def top_step(t):
        m = t - jnp.where(delta == 0, 0, TOP_LAG + SKEW * top_depth)
        slot = jnp.clip(m, 0, TOP_PARTS - 1)
        piece = top.at[q, pl.ds(pl.multiple_of(slot * TOP_ROWS, TOP_ROWS), TOP_ROWS), :]

        def go(kind, offset):
            send(piece, piece, top_send.at[kind], top_recv.at[q, slot], top_to(offset)).start()

        @pl.when((m >= 0) & (m < TOP_PARTS))
        def _():
            @pl.when(delta > 0)
            def _():
                send(piece, piece, top_send.at[0], top_recv.at[q, slot], here).wait_recv()

            for kind, offset in enumerate((2, -2, -1, 1)):
                pl.when(top_goes[kind])(lambda kind=kind, offset=offset: go(kind, offset))

    def hops(p):
        return jnp.where(p == 0, 0, jnp.where(p == 2, 2, 1))

    def tree_step(t):
        for h in range(2):
            u, v = (x, y) if h == 0 else (y, x)
            p = jnp.where(v == 0, u, v)
            late = (u == 0) & (v != 0)

            def at(u2, v2):
                x2, y2 = (u2, v2) if h == 0 else (v2, u2)
                return (row, x2 * 8 + y2 * 2 + core)

            m = t - SKEW * (jnp.where(late, 2, hops(u)) + hops(v))
            slot = jnp.clip(m, 0, TREE_PARTS - 1)
            start = 128 * h + TREE_ROWS * lax.rem(slot, TREE_PARTS // 6)
            part = panel.at[core, slot // (TREE_PARTS // 6), pl.ds(pl.multiple_of(start, TREE_ROWS), TREE_ROWS), :]
            half0 = panel.at[core, slot // (TREE_PARTS // 6), pl.ds(pl.multiple_of(start, TREE_ROWS // 2), TREE_ROWS // 2), :]
            half1 = panel.at[core, slot // (TREE_PARTS // 6), pl.ds(pl.multiple_of(start + TREE_ROWS // 2, TREE_ROWS // 2), TREE_ROWS // 2), :]

            def go(piece, kind, half, device):
                send(piece, piece, tree_send.at[h, kind], tree_recv.at[h, slot, half], device).start()

            @pl.when((m >= 0) & (m < TREE_PARTS))
            def _():
                @pl.when(((p == 1) | (p == 3)) & jnp.logical_not(late))
                def _():
                    send(part, part, tree_send.at[h, 0], tree_recv.at[h, slot, 0], here).wait_recv()

                @pl.when((p == 2) | late)
                def _():
                    send(half0, half0, tree_send.at[h, 0], tree_recv.at[h, slot, 0], here).wait_recv()
                    send(half1, half1, tree_send.at[h, 0], tree_recv.at[h, slot, 1], here).wait_recv()

                @pl.when((v == 0) & (u == 0))
                def _():
                    go(part, 0, 0, at(1, 0))
                    go(part, 1, 0, at(3, 0))

                @pl.when((p == 1) & jnp.logical_not(late))
                def _():
                    go(half0, 2, 0, at(jnp.where(v == 0, 2, u), jnp.where(v == 0, 0, 2)))

                @pl.when((p == 3) & jnp.logical_not(late))
                def _():
                    go(half1, 2, 1, at(jnp.where(v == 0, 2, u), jnp.where(v == 0, 0, 2)))

                @pl.when((v == 0) & (u != 0))
                def _():
                    go(part, 3, 0, at(u, 1))
                    go(part, 4, 0, at(u, 3))

                @pl.when((v != 0) & (u == 1))
                def _():
                    go(half0, 5, 0, at(0, v))

                @pl.when((v != 0) & (u == 3))
                def _():
                    go(half1, 5, 1, at(0, v))

                send(part, part, pair_send.at[h], pair_recv.at[h], twin).start()

    def tick(t):
        top_step(t)
        tree_step(t)

    def ticks(start, stop):
        def one(t, carry):
            tick(t)
            return carry
        lax.fori_loop(start, stop, one, 0)

    pieces = (
        (first_piece(chip), 0, 0),
        (low.at[chip, pl.ds(0, 8), :], 0, 0),
        (low.at[chip, pl.ds(8, 16), :], 1, 0),
        (high.at[chip], 1, 1),
    )
    def scattered(n):
        piece, start, carrier = pieces[n]

        @pl.when((row == start) & (core == carrier) & (chip != 0))
        def _():
            send(piece, piece, scatter_send.at[n], scatter_recv.at[n], here).wait_recv()

    def along_ring(n):
        piece, start, carrier = pieces[n]

        @pl.when((row == start) & (core == carrier))
        def _():
            loop(15, lambda j: send(piece, piece, ring_send.at[n], ring_recv.at[n], (ring_peer(j), col)).start())

    def ring_arrived(n):
        piece, start, _ = pieces[n]

        @pl.when(row != start)
        def _():
            send(piece, piece, ring_send.at[n], ring_recv.at[n], here).wait_recv()

    def gather_first():
        loop(15, lambda j: send(
            first_piece(chip), first_piece(chip), plane_send.at[0], plane_recv.at[0],
            (row, plane_peer(j) * 2)).start())

    pl.when(row >= 2)(lambda: ticks(0, FAR_TICKS))
    scattered(0)
    pl.when((row == 0) & (core == 0))(gather_first)
    for n in range(4):
        if n:
            scattered(n)
        along_ring(n)
    pl.when(row < 2)(lambda: ticks(0, NEAR_TICKS))

    @pl.when((row != 0) & (core == 0))
    def _():
        ring_arrived(0)
        gather_first()

    pl.when(row < 2)(lambda: ticks(NEAR_TICKS, FAR_TICKS))
    ticks(FAR_TICKS, MID_TICKS)

    @pl.when(core == 0)
    def _():
        ring_arrived(1)
        ring_arrived(2)
        loop(15, lambda j: send(
            low.at[chip], low.at[chip], plane_send.at[1], plane_recv.at[1], (row, plane_peer(j) * 2)).start())

    @pl.when(core == 1)
    def _():
        ring_arrived(3)
        loop(15, lambda j: send(
            high.at[chip], high.at[chip], plane_send.at[2], plane_recv.at[2],
            (row, plane_peer(j) * 2 + 1)).start())

    ticks(MID_TICKS, EARLY)

    @pl.when(core == 0)
    def _():
        send(first.at[pl.ds(0, 120), :], first.at[pl.ds(0, 120), :], plane_send.at[0], plane_recv.at[0], here).wait_recv()
        send(first, first, twin_send.at[0], twin_recv.at[0], twin).start()

    @pl.when(core == 1)
    def _():
        send(first, first, twin_send.at[0], twin_recv.at[0], here).wait_recv()

    def rest_in_plane():
        @pl.when(core == 0)
        def _():
            send(low.at[pl.ds(0, 15)], low.at[pl.ds(0, 15)], plane_send.at[1], plane_recv.at[1], here).wait_recv()
            send(low, low, twin_send.at[1], twin_recv.at[1], twin).start()

        @pl.when(core == 1)
        def _():
            send(high.at[pl.ds(0, 15)], high.at[pl.ds(0, 15)], plane_send.at[2], plane_recv.at[2], here).wait_recv()
            send(high, high, twin_send.at[2], twin_recv.at[2], twin).start()

    def rest_from_twin():
        @pl.when(core == 1)
        def _():
            send(low, low, twin_send.at[1], twin_recv.at[1], here).wait_recv()

        @pl.when(core == 0)
        def _():
            send(high, high, twin_send.at[2], twin_recv.at[2], here).wait_recv()

        for i in range(16):
            a[SB + 8 * i:SB + 8 * i + 8, 0:NB] = low[i, 0:8, :]
            a[NB + 16 * i:NB + 16 * i + 16, 0:NB] = low[i, 8:24, :]
            a[NB + 16 * i:NB + 16 * i + 16, NB:2 * NB] = high[i]

    a[0:SB, 0:SB] = first[...]

    def hook(s, k):
        if k == 7:
            pl.when(s == 0)(rest_in_plane)
        if k in TICKS:
            tick(EARLY + len(TICKS) * s + TICKS.index(k))

    def unpack(s):
        pl.when(s == 0)(rest_from_twin)

    factor(a, m, z, lb, xs, hook, unpack)

    def top_arrived(m):
        piece = top.at[1 - q, pl.ds(pl.multiple_of(m * TOP_ROWS, TOP_ROWS), TOP_ROWS), :]
        send(piece, piece, top_send.at[0], top_recv.at[1 - q, m], here).wait_recv()

    @pl.when((row != 0) | (q != 1))
    def _():
        loop(TOP_PARTS, top_arrived)

    sq_r = lax.broadcasted_iota(jnp.int32, (NB, NB), 0)
    sq_c = lax.broadcasted_iota(jnp.int32, (NB, NB), 1)
    pick = jnp.where(sq_r == sq_c, -1.0, 0.0)
    upper = dot3(z[0:NB, 0:NB], top[0], 1)
    under = dot3(z[NB:2 * NB, 0:NB], top[0], 1) + dot3(z[NB:2 * NB, NB:2 * NB], top[1], 1)
    upper = jnp.where(is_root, jnp.where(col == 0, pick, 0.0), upper)
    under = jnp.where(is_root, jnp.where(col == 1, pick, 0.0), under)
    w_hi[0:NB], w_lo[0:NB] = halves(dot3(z[0:NB, 0:NB], upper, 0) + dot3(z[NB:2 * NB, 0:NB], under, 0))
    w_hi[NB:2 * NB], w_lo[NB:2 * NB] = halves(dot3(z[NB:2 * NB, NB:2 * NB], under, 0))

    for h in range(2):
        part = panel.at[1 - core, :, pl.ds(128 * h, 128), :]
        send(part, part, pair_send.at[h], pair_recv.at[h], here).wait_recv()

    for g in range(6):
        index = g * N_ROW + row
        value = jnp.where(is_root, 0.0, own[g])
        for k in range(2):
            hi, lo = halves(panel[k, g])
            w1, w2 = w_hi[NB * k:NB * k + NB], w_lo[NB * k:NB * k + NB]
            value = value - (dot16(hi, w1) + (dot16(hi, w2) + dot16(lo, w1)))
        keep = (index > col) | ((index == col) & ((sq_r >= sq_c) | jnp.logical_not(is_root)))
        o_ref[g] = jnp.where(keep, value, 0.0)

    def sent(ref, sem):
        send(ref, ref, sem, own_sem, here).wait_send()

    for n, holds, ref in (
        (0, holds_00, first.at[pl.ds(0, 120), :]),
        (1, holds_00, low.at[pl.ds(0, 15), pl.ds(0, 8), :]),
        (2, holds_10, low.at[pl.ds(0, 15), pl.ds(8, 16), :]),
        (3, holds_11, high.at[pl.ds(0, 15)]),
    ):
        pl.when(holds)(lambda n=n, ref=ref: sent(ref, scatter_send.at[n]))
        pl.when((row == pieces[n][1]) & (core == pieces[n][2]))(lambda n=n, ref=ref: sent(ref, ring_send.at[n]))

    @pl.when(core == 0)
    def _():
        sent(first.at[pl.ds(0, 120), :], plane_send.at[0])
        sent(low.at[pl.ds(0, 15)], plane_send.at[1])
        sent(first, twin_send.at[0])
        sent(low, twin_send.at[1])

    @pl.when(core == 1)
    def _():
        sent(high.at[pl.ds(0, 15)], plane_send.at[2])
        sent(high, twin_send.at[2])

    for kind in range(4):
        pl.when(top_goes[kind])(lambda kind=kind: sent(top.at[0], top_send.at[kind]))

    for h in range(2):
        u, v = (x, y) if h == 0 else (y, x)
        p = jnp.where(v == 0, u, v)
        whole = panel.at[core, :, pl.ds(0, 128), :]
        half = panel.at[core, :, pl.ds(0, 64), :]

        @pl.when((v == 0) & (u == 0))
        def _():
            sent(whole, tree_send.at[h, 0])
            sent(whole, tree_send.at[h, 1])

        pl.when(((p == 1) | (p == 3)) & ((v == 0) | (u != 0)))(lambda: sent(half, tree_send.at[h, 2]))
        pl.when((v != 0) & ((u == 1) | (u == 3)))(lambda: sent(half, tree_send.at[h, 5]))

        @pl.when((v == 0) & (u != 0))
        def _():
            sent(whole, tree_send.at[h, 3])
            sent(whole, tree_send.at[h, 4])

        sent(whole, pair_send.at[h])


def on_device(slab):
    dma = pltpu.SemaphoreType.DMA
    return pl.pallas_call(
        kernel,
        out_shape=jax.ShapeDtypeStruct(slab.shape, jnp.float32),
        in_specs=[pl.BlockSpec(memory_space=pl.ANY)],
        out_specs=pl.BlockSpec(memory_space=pltpu.VMEM),
        scratch_shapes=[
            pltpu.VMEM((6, NB, NB), jnp.float32),
            pltpu.VMEM((SB, SB), jnp.float32),
            pltpu.VMEM((16, 24, NB), jnp.float32),
            pltpu.VMEM((16, 16, NB), jnp.float32),
            pltpu.VMEM((2, NB, NB), jnp.float32),
            pltpu.VMEM((2, 6, NB, NB), jnp.float32),
            pltpu.VMEM((768, 768), jnp.float32),
            pltpu.VMEM((768, 512), jnp.float32),
            pltpu.VMEM((512, 512), jnp.float32),
            pltpu.VMEM((3, SB, SB), jnp.float32),
            pltpu.VMEM((SB, SB), jnp.float32),
            pltpu.VMEM((512, NB), jnp.bfloat16),
            pltpu.VMEM((512, NB), jnp.bfloat16),
            dma, dma((4,)), dma((4,)), dma((4,)), dma((4,)), dma((3,)), dma((3,)), dma((3,)), dma((3,)),
            dma((4,)), dma((2, TOP_PARTS)), dma((2, 6)), dma((2, TREE_PARTS, 2)), dma((2,)), dma((2,)),
        ],
        compiler_params=pltpu.CompilerParams(
            collective_id=0, has_side_effects=True, vmem_limit_bytes=VMEM
        ),
    )(slab)


def solution(mesh):
    spec = P(None, "row", "col")
    return jax.shard_map(on_device, mesh=mesh, in_specs=(spec,), out_specs=spec, check_vma=False)
```
